32 devices in a mesh: grp: 2 (over x), lat: 16 (over z, y, core).
Axes of the slice: x: 2, y: 2, z: 4, core: 2. Of those that a mesh axis runs over, the one named last changes fastest.
Arguments:
- activations: bfloat16 [4096, 4096], P(('grp', 'lat')), parts along dimension 0, may hold values from -162 to 162
- block_ids: int32 [4096, 2], P(('grp', 'lat')), parts along dimension 0, may hold values from 0 to 63, all different within a row; in each aligned block of 128 rows (0 to 127, 128 to 255, ...) at most 6 rows name the same one
- enc_weight: bfloat16 [4096, 4096], P(None, 'lat'), may hold values from -0.09375 to 0.09375
- enc_bias: float32 [4096], P('lat'), may hold values from -3 to 3
- dec_weight: bfloat16 [4096, 4096], P('lat'), may hold values from -0.5 to 0.5
- dec_bias: float32 [4096], replicated, may hold values from -3 to 3
Outputs:
- rebuilt: bfloat16 [4096, 4096], P(('grp', 'lat')), parts along dimension 0
- enc_grad: bfloat16 [8192, 4096], P('grp', 'lat'), parts along dimension 0
- dec_grad: bfloat16 [8192, 4096], P(('grp', 'lat')), parts along dimension 0
- bias_grad: float32 [8192], P(('grp', 'lat')), parts along dimension 0
The draws below stay inside these ranges and needn't reach their ends.
There are 2 independent parts, one for each index of `grp`. The reference program is written for one: setup_inputs(seed, part) draws one part's arguments, and reference() takes and returns one part's arrays. A program takes and returns all parts, laid end to end along the dimension named above; an argument that names none is the same for every part. Nothing has to cross between parts.
Inputs may be any that keep to these rules, and one draw needn't show every extreme that they name: `block_ids`: within each token's row the 2 blocks differ. Among the 128 tokens of one index of lat no block is named by more than 6 tokens, and some block is named by exactly 6.
All inputs are finite; a program needn't handle non-finite values.
Results may differ from the reference program's by a relative error of at most 0.0058.
Values may be sent and summed in bfloat16 or wider, within the bound.
No kernel may reach another device: no remote copies, remote signals or barrier semaphores. Data moves between devices by JAX's collectives and lax.ppermute only.
A program may use at most 128 MiB of HBM per device.

```python
import math
import jax
import jax.numpy as jnp
import numpy as np
from jax import lax

D = 4096
BLOCK = 64
K_BLK = 2
TOK_DEV = 128
NBLK = 64
LATENTS = 4096
TOKENS = 2048
MOST = 6
N_LAT = 16


def draw_activations(key, part):
    key = jax.random.fold_in(key, 11)
    key_base, key_row, key_col = jax.random.split(key, 3)
    position = (jnp.arange(TOKENS, dtype=jnp.float32) / TOKENS)[:, None]
    row_level = jax.random.uniform(key_row, (TOKENS, 1), jnp.float32)
    col_level = jax.random.uniform(key_col, (1, D), jnp.float32)
    row_scale = 0.3 * jnp.power(10.0, row_level)
    col_scale = 0.3 * jnp.power(10.0, col_level)
    base = jnp.clip(jax.random.normal(key_base, (TOKENS, D), jnp.float32), -6.0, 6.0)
    rising = jnp.power(1.7320508, position)
    return (base * row_scale * col_scale * rising).astype(jnp.bfloat16)


def block_scale(own_key, extent, cuts, low, largest):
    def one(dim, blocks):
        steps = jax.random.uniform(jax.random.fold_in(jax.random.fold_in(own_key, 6), dim), (blocks,), jnp.float32, low / len(cuts), largest / len(cuts))
        return jnp.repeat(jnp.exp(steps), extent[dim] // blocks).reshape((-1,) + (1,) * (len(extent) - dim - 1))

    factor_of = one(*cuts[0])
    for cut in cuts[1:]:
        factor_of = factor_of * one(*cut)
    return factor_of


def deal_out(rng, own, number, rows, amount, top, bound, skew):
    sequence = jax.random.permutation(rng, amount)
    crowded, usual = portions_of(amount, rows * top, bound, skew, True), portions_of(amount, rows * top, bound, skew, False)
    places = jnp.arange(amount)

    def named(tallies, offset_by):
        used = int((tallies > 0).sum())
        fixed = max(1, used // 4)
        moved = fixed + (places - fixed + offset_by * (used - fixed)) % max(1, amount - fixed)
        return jnp.zeros((amount,), jnp.int32).at[sequence[jnp.where(places < fixed, places, moved)]].set(jnp.asarray(tallies, jnp.int32))

    tallies = jnp.where(number % 4 == 0, named(crowded, number // 4), named(usual, number - number // 4 - 1))
    mixed = jax.random.permutation(jax.random.fold_in(own, 3), amount)
    giver, receiver = mixed[0:amount // 2 * 2:2], mixed[1:amount // 2 * 2:2]
    margin = jnp.minimum(tallies[giver] - 1, bound - tallies[receiver]) // 2
    margin = jnp.where((giver == sequence[0]) | (receiver == sequence[0]) | (tallies[receiver] == 0), 0, jnp.maximum(margin, 0))
    moved = jax.random.randint(jax.random.fold_in(own, 4), (amount // 2,), 0, 1 << 20) % (margin + 1)
    tallies = tallies.at[giver].add(-moved).at[receiver].add(moved)
    items = jnp.searchsorted(jnp.cumsum(tallies), jnp.arange(rows * top), side="right").astype(jnp.int32)
    grid = items.reshape(top, rows).T
    grid = grid[jax.random.permutation(jax.random.fold_in(own, 1), rows)]
    offset_by = jax.random.randint(jax.random.fold_in(own, 2), (rows, 1), 0, top)
    return jnp.take_along_axis(grid, (jnp.arange(top)[None, :] + offset_by) % top, axis=1)


def portions_of(count, total, most, skew, full):
    loads = [(1 << 20) // math.isqrt(rank ** skew) + 1 for rank in range(1, count + 1)]
    largest = most if full else min(most, max(-(-total // count), total * loads[0] // sum(loads)))
    least = 1 if total - largest >= count - 1 else 0
    given, rest = [largest] + [least] * (count - 1), total - largest - least * (count - 1)
    while rest > 0:
        movable = [i for i in range(1, count) if given[i] < largest] or [i for i in range(1, count) if given[i] < most]
        whole, budget = sum([loads[i] for i in movable]), rest
        for i in movable:
            more = min(most - given[i], max(1, budget * loads[i] // whole), rest)
            given[i] = given[i] + more
            rest = rest - more
    return np.array(given)


def noise(key, dims, deviation, limit, pieces=(), kind=jnp.bfloat16):
    level = block_scale(key, dims, pieces, -0.22, 0.18) if pieces else 1.0
    drawn = jax.random.normal(key, dims, jnp.float32) * deviation * level
    return jnp.minimum(jnp.maximum(drawn, -limit), limit).astype(kind)


def setup_inputs(seed: int = 0, part: int = 0) -> dict:
    streams_of = jax.random.split(jax.random.key(seed), 7)
    part_splits = jax.random.split(jax.random.fold_in(streams_of[6], part), 7)
    activations = draw_activations(jax.random.fold_in(jax.random.fold_in(streams_of[6], part), 71), part)
    block_ids_keys = jax.random.split(jax.random.fold_in(part_splits[1], 1), TOKENS // TOK_DEV)
    block_ids_turns = jax.random.permutation(jax.random.fold_in(part_splits[1], 3), TOKENS // TOK_DEV)
    block_ids = jax.vmap(lambda own, number: deal_out(jax.random.fold_in(part_splits[1], 2), own, number, TOK_DEV, NBLK, K_BLK, MOST, 2))(block_ids_keys, block_ids_turns).reshape((TOKENS, K_BLK))
    enc_weight = noise(streams_of[2], (D, LATENTS), D ** -0.5, 0.09375, ((1, 16),))
    enc_bias = noise(streams_of[3], (LATENTS,), 0.5, 3.0, ((0, 16),), jnp.float32)
    dec_weight = noise(streams_of[4], (LATENTS, D), (K_BLK * BLOCK) ** -0.5, 0.5, ((0, 16),))
    dec_bias = noise(streams_of[5], (D,), 0.5, 3.0, (), jnp.float32)
    return dict(activations=activations, block_ids=block_ids, enc_weight=enc_weight, enc_bias=enc_bias, dec_weight=dec_weight, dec_bias=dec_bias)


LOSS_SCALE = 0.5


def activate(preact):
    inner_arg = 0.7978845608 * (preact + 0.044715 * preact * preact * preact)
    tangent = jnp.tanh(inner_arg)
    output = 0.5 * preact * (1.0 + tangent)
    slopes = 0.5 * (1.0 + tangent) + 0.5 * preact * (1.0 - tangent * tangent) * 0.7978845608 * (1.0 + 0.134145 * preact * preact)
    return output, slopes


def reference(activations, block_ids, enc_weight, enc_bias, dec_weight, dec_bias):
    nblocks = LATENTS // BLOCK
    per_device = block_ids.reshape(N_LAT, TOK_DEV * K_BLK)
    block_iota = jnp.arange(nblocks, dtype=jnp.int32)
    onehot = (per_device[:, :, None] == block_iota[None, None, :]).astype(jnp.int32)
    slot_rank = jnp.sum(onehot * (jnp.cumsum(onehot, axis=1) - 1), axis=2)
    device_iota = jnp.arange(N_LAT, dtype=jnp.int32)[:, None]
    slot_flat = ((per_device * N_LAT + device_iota) * MOST + slot_rank).reshape(-1).astype(jnp.int32)
    owners = jnp.arange(TOKENS * K_BLK, dtype=jnp.int32) // K_BLK
    span_all = N_LAT * MOST
    token_of = jnp.zeros((nblocks * span_all,), jnp.int32).at[slot_flat].set(owners).reshape(nblocks, span_all)
    filled = jnp.zeros((nblocks * span_all,), jnp.int32).at[slot_flat].set(1).reshape(nblocks, span_all)
    mean_square = jnp.mean(jnp.square(activations.astype(jnp.float32))) + 1e-6

    def block_codes(block_index):
        gathered = activations[token_of[block_index]]
        enc_cols = lax.dynamic_slice_in_dim(enc_weight, block_index * BLOCK, BLOCK, 1)
        bias_cols = lax.dynamic_slice_in_dim(enc_bias, block_index * BLOCK, BLOCK, 0)
        preact = jnp.dot(gathered, enc_cols, preferred_element_type=jnp.float32) + bias_cols[None, :]
        output, slopes = activate(preact)
        dec_rows = lax.dynamic_slice_in_dim(dec_weight, block_index * BLOCK, BLOCK, 0)
        return gathered, output.astype(jnp.bfloat16), slopes, dec_rows

    def forward(running, block_index):
        gathered, code_rows, slopes, dec_rows = block_codes(block_index)
        partial_value = jnp.dot(code_rows, dec_rows, preferred_element_type=jnp.float32).astype(jnp.bfloat16)
        partial_value = lax.optimization_barrier(partial_value).astype(jnp.float32)
        live = filled[block_index].astype(jnp.float32)[:, None]
        running = running.at[token_of[block_index]].add(partial_value * live)
        return running, None

    start = jnp.zeros((TOKENS, D), jnp.float32) + dec_bias[None, :].astype(jnp.float32)
    full, _unused = lax.scan(forward, start, jnp.arange(nblocks, dtype=jnp.int32))
    errors = (LOSS_SCALE * (full - activations.astype(jnp.float32)) / mean_square).astype(jnp.bfloat16)

    def backward(running, block_index):
        gathered, code_rows, slopes, dec_rows = block_codes(block_index)
        live = filled[block_index][:, None] > 0
        err_rows = jnp.where(live, errors[token_of[block_index]], jnp.zeros((), jnp.bfloat16))
        code_grad = jnp.dot(err_rows, dec_rows.T, preferred_element_type=jnp.float32) * slopes
        enc_part = jnp.dot(gathered.T, code_grad.astype(jnp.bfloat16), preferred_element_type=jnp.float32).astype(jnp.bfloat16)
        dec_part = jnp.dot(code_rows.T, err_rows, preferred_element_type=jnp.float32).astype(jnp.bfloat16)
        return running, (enc_part, dec_part, jnp.sum(code_grad, axis=0))

    _other, stacked = lax.scan(backward, jnp.zeros((), jnp.float32), jnp.arange(nblocks, dtype=jnp.int32))
    enc_grad = stacked[0].transpose(1, 0, 2).reshape(D, LATENTS)
    dec_grad = stacked[1].reshape(LATENTS, D)
    bias_grad = stacked[2].reshape(LATENTS)
    return full.astype(jnp.bfloat16), enc_grad, dec_grad, bias_grad
```

```python
import jax
import jax.numpy as jnp
from jax import lax
from jax.sharding import PartitionSpec as P

BLOCK = 64
LOSS_SCALE = 0.5
F32 = jnp.float32
BF16 = jnp.bfloat16


def activate(preact):
    inner_arg = 0.7978845608 * (preact + 0.044715 * preact * preact * preact)
    tangent = jnp.tanh(inner_arg)
    output = 0.5 * preact * (1.0 + tangent)
    slopes = 0.5 * (1.0 + tangent) + 0.5 * preact * (1.0 - tangent * tangent) * 0.7978845608 * (
        1.0 + 0.134145 * preact * preact
    )
    return (output, slopes)


def dot(left, right, left_dim, right_dim):
    dims = (((left_dim,), (right_dim,)), ((), ()))
    return lax.dot_general(left, right, dims, preferred_element_type=F32)


def exchange(rows):
    return lax.all_to_all(rows, "lat", split_axis=0, concat_axis=0, tiled=True)


def per_device(activations, block_ids, enc_weight, enc_bias, dec_weight, dec_bias):
    tok_rows, feature_dim = activations.shape
    active_count = block_ids.shape[1]
    lat_devices = lax.axis_size("lat")
    local_latents = enc_weight.shape[1]
    blocks_dev = local_latents // BLOCK
    nblocks = blocks_dev * lat_devices
    capacity = max(2, 3 * tok_rows * active_count // (2 * nblocks))
    slot_total = nblocks * capacity

    flat_ids = block_ids.reshape(-1)
    pairs = flat_ids.shape[0]
    order = jnp.arange(pairs, dtype=jnp.int32)
    same = (flat_ids[:, None] == flat_ids[None, :]) & (order[None, :] < order[:, None])
    slot_of = flat_ids * capacity + jnp.sum(same.astype(jnp.int32), axis=1)
    slot_of = slot_of.reshape(tok_rows, active_count)
    slots = jnp.arange(slot_total, dtype=jnp.int32)
    select = jnp.any(slots[:, None, None] == slot_of[None, :, :], axis=2).astype(BF16)

    squares = jnp.sum(jnp.square(activations.astype(F32)))
    squares = lax.all_gather(jnp.full((8, 128), squares, F32), "lat", axis=0, tiled=True)
    square_sum = jnp.sum(squares.reshape(lat_devices, 8, 128)[:, 0, 0])
    mean_square = square_sum / (tok_rows * lat_devices * feature_dim) + 1e-06
    scale = LOSS_SCALE / mean_square

    send_rows = dot(select, activations, 1, 0).astype(BF16)
    received = exchange(send_rows)
    row_block = (slots % (blocks_dev * capacity)) // capacity
    own = row_block[:, None] == (jnp.arange(local_latents, dtype=jnp.int32) // BLOCK)[None, :]
    preact = dot(received, enc_weight, 1, 0) + enc_bias[None, :]
    output, slopes = activate(preact)
    code_rows = jnp.where(own, output, 0.0).astype(BF16)
    slopes = jnp.where(own, slopes, 0.0)
    partial_value = dot(code_rows, dec_weight, 1, 0).astype(BF16)
    returned = exchange(partial_value)
    full = dec_bias[None, :] + dot(select, returned, 0, 0)
    errors = (full - activations.astype(F32)).astype(BF16)
    err_rows = dot(select, errors, 1, 0).astype(BF16)
    got_errors = exchange(err_rows)
    code_grad = dot(got_errors, dec_weight, 1, 1) * (slopes * scale)
    bias_grad = jnp.sum(code_grad, axis=0)
    enc_grad = dot(received, code_grad.astype(BF16), 0, 0).astype(BF16)
    dec_grad = (dot(code_rows, got_errors, 0, 0) * scale).astype(BF16)
    return (full.astype(BF16), enc_grad, dec_grad, bias_grad)


def solution(mesh):
    return jax.shard_map(
        per_device,
        mesh=mesh,
        in_specs=(
            P(("grp", "lat"), None),
            P(("grp", "lat"), None),
            P(None, "lat"),
            P("lat"),
            P("lat", None),
            P(),
        ),
        out_specs=(
            P(("grp", "lat"), None),
            P("grp", "lat"),
            P(("grp", "lat"), None),
            P(("grp", "lat")),
        ),
        check_vma=False,
    )
```

```python
import jax
import jax.numpy as jnp
from jax import lax
from jax.sharding import PartitionSpec as P

BLOCK = 64
LOSS_SCALE = 0.5
CHUNKS = 2
F32 = jnp.float32
BF16 = jnp.bfloat16


def activate(preact):
    inner_arg = 0.7978845608 * (preact + 0.044715 * preact * preact * preact)
    tangent = jnp.tanh(inner_arg)
    output = 0.5 * preact * (1.0 + tangent)
    slopes = 0.5 * (1.0 + tangent) + 0.5 * preact * (1.0 - tangent * tangent) * 0.7978845608 * (
        1.0 + 0.134145 * preact * preact
    )
    return (output, slopes)


def dot(left, right, left_dim, right_dim):
    dims = (((left_dim,), (right_dim,)), ((), ()))
    return lax.dot_general(left, right, dims, preferred_element_type=F32)


def together(*values):
    return lax.optimization_barrier(values)


def per_device(activations, block_ids, enc_weight, enc_bias, dec_weight, dec_bias):
    tok_rows, feature_dim = activations.shape
    active_count = block_ids.shape[1]
    devices = lax.axis_size("lat")
    half = devices // 2
    local_latents = enc_weight.shape[1]
    blocks_dev = local_latents // BLOCK
    nblocks = blocks_dev * devices
    capacity = max(2, 3 * tok_rows * active_count // (2 * nblocks))
    half_slots = half * blocks_dev * capacity
    width = feature_dim // CHUNKS
    halves = [list(range(half)), list(range(half, devices))]

    def exchange(rows):
        return lax.all_to_all(
            rows, "lat", split_axis=0, concat_axis=0, axis_index_groups=halves, tiled=True
        )

    def swap(rows, step=half):
        return lax.ppermute(rows, "lat", [(i, i ^ step) for i in range(devices)])

    def cut(rows):
        return [rows[:, i * width : (i + 1) * width] for i in range(CHUNKS)]

    def pick(select, rows):
        return dot(select, rows, 1, 0).astype(BF16)

    flat_ids = block_ids.reshape(-1)
    pairs = flat_ids.shape[0]
    order = jnp.arange(pairs, dtype=jnp.int32)
    same = (flat_ids[:, None] == flat_ids[None, :]) & (order[None, :] < order[:, None])
    slot_of = flat_ids * capacity + jnp.sum(same.astype(jnp.int32), axis=1)
    slot_of = slot_of.reshape(tok_rows, active_count).T
    my_half = lax.axis_index("lat") // half
    slots = jnp.arange(half_slots, dtype=jnp.int32)

    def selection(slot):
        slot = slot - my_half * half_slots
        return jnp.any(slots[:, None, None] == slot[None, :, :], axis=1).astype(BF16)

    squares = jnp.full((8, 128), jnp.sum(jnp.square(activations.astype(F32))), F32)
    steps = [1 << i for i in range((devices - 1).bit_length())]

    def more(squares):
        return squares + swap(squares, steps.pop(0)) if steps else squares

    act_cut = cut(activations)
    slot_held = swap(slot_of)
    held_0 = swap(act_cut[0])
    sel_own = selection(slot_of)
    got_own = exchange(pick(sel_own, activations))
    held_0, slot_held, got_own, squares = together(held_0, slot_held, got_own, more(squares))
    sel_held = selection(slot_held)
    held_1 = swap(act_cut[1])
    got_0 = exchange(pick(sel_held, held_0))
    held_1, got_0, squares = together(held_1, got_0, more(squares))
    got_1 = exchange(pick(sel_held, held_1))
    got_1, squares = together(got_1, more(squares))
    got_held = [got_0, got_1]

    row_block = (slots % (blocks_dev * capacity)) // capacity
    own = row_block[:, None] == (jnp.arange(local_latents, dtype=jnp.int32) // BLOCK)[None, :]

    def encode(preact):
        output, slopes = activate(preact + enc_bias[None, :])
        return jnp.where(own, output, 0.0).astype(BF16), jnp.where(own, slopes, 0.0)

    enc_cut = [enc_weight[i * width : (i + 1) * width] for i in range(CHUNKS)]
    dec_cut = cut(dec_weight)
    code_own, slope_own = encode(dot(got_own, enc_weight, 1, 0))
    code_held, slope_held = encode(sum(dot(a, b, 1, 0) for a, b in zip(got_held, enc_cut)))

    back_0 = exchange(dot(code_held, dec_cut[0], 1, 0).astype(BF16))
    back_0, code_held, code_own, squares = together(back_0, code_held, code_own, more(squares))
    while steps:
        squares = more(squares)
    far_0 = swap(dot(sel_held, back_0, 0, 0).astype(BF16))
    back_1 = exchange(dot(code_held, dec_cut[1], 1, 0).astype(BF16))
    far_0, back_1, code_own = together(far_0, back_1, code_own)
    far_1 = swap(dot(sel_held, back_1, 0, 0).astype(BF16))
    back_own = exchange(dot(code_own, dec_weight, 1, 0).astype(BF16))
    far_1, back_own = together(far_1, back_own)

    full = dec_bias[None, :] + dot(sel_own, back_own, 0, 0)
    full = full + jnp.concatenate([far_0, far_1], axis=1).astype(F32)
    errors = (full - activations.astype(F32)).astype(BF16)
    err_cut = cut(errors)
    far_0 = swap(err_cut[0])
    err_own = exchange(pick(sel_own, errors))
    far_0, err_own = together(far_0, err_own)
    far_1 = swap(err_cut[1])
    err_0 = exchange(pick(sel_held, far_0))
    far_1, err_0 = together(far_1, err_0)
    err_1 = exchange(pick(sel_held, far_1))
    err_held = [err_0, err_1]
    mean_square = squares[0, 0] / (tok_rows * devices * feature_dim) + 1e-06
    scale = LOSS_SCALE / mean_square

    grad_own = dot(err_own, dec_weight, 1, 1) * (slope_own * scale)
    grad_held = sum(dot(a, b, 1, 1) for a, b in zip(err_held, dec_cut)) * (slope_held * scale)
    bias_grad = jnp.sum(grad_own, axis=0) + jnp.sum(grad_held, axis=0)
    grad_own, grad_held = grad_own.astype(BF16), grad_held.astype(BF16)
    enc_grad = [
        (dot(a[:, i * width : (i + 1) * width], grad_own, 0, 0) + dot(b, grad_held, 0, 0)).astype(BF16)
        for i, (a, b) in enumerate(zip([got_own] * CHUNKS, got_held))
    ]
    dec_grad = [
        ((dot(code_own, a, 0, 0) + dot(code_held, b, 0, 0)) * scale).astype(BF16)
        for a, b in zip(cut(err_own), err_held)
    ]
    return (
        full.astype(BF16),
        jnp.concatenate(enc_grad, axis=0),
        jnp.concatenate(dec_grad, axis=1),
        bias_grad,
    )


def solution(mesh):
    return jax.shard_map(
        per_device,
        mesh=mesh,
        in_specs=(
            P(("grp", "lat"), None),
            P(("grp", "lat"), None),
            P(None, "lat"),
            P("lat"),
            P("lat", None),
            P(),
        ),
        out_specs=(
            P(("grp", "lat"), None),
            P("grp", "lat"),
            P(("grp", "lat"), None),
            P(("grp", "lat")),
        ),
        check_vma=False,
    )
```

```python
import jax
import jax.numpy as jnp
from jax import lax
from jax.experimental import pallas as pl
from jax.experimental.pallas import tpu as pltpu
from jax.sharding import PartitionSpec as P

BLOCK = 64
LOSS_SCALE = 0.5
F32 = jnp.float32
BF16 = jnp.bfloat16


def activate(preact):
    inner_arg = 0.7978845608 * (preact + 0.044715 * preact * preact * preact)
    tangent = jnp.tanh(inner_arg)
    output = 0.5 * preact * (1.0 + tangent)
    slopes = 0.5 * (1.0 + tangent) + 0.5 * preact * (1.0 - tangent * tangent) * 0.7978845608 * (
        1.0 + 0.134145 * preact * preact
    )
    return (output, slopes)


def dot(left, right, left_dim, right_dim):
    dims = (((left_dim,), (right_dim,)), ((), ()))
    return lax.dot_general(left, right, dims, preferred_element_type=F32)


def together(*values):
    return lax.optimization_barrier(values)


def squares_kernel(rows_ref, total_ref):
    total = jnp.zeros((8, 128), F32)
    rows, columns = rows_ref.shape
    for i in range(0, columns, 128):
        part = rows_ref[:, i : i + 128].astype(F32)
        total = total + jnp.sum((part * part).reshape(rows // 8, 8, 128), axis=0)
    total_ref[...] = jnp.full((8, 128), jnp.sum(total), F32)


def sum_of_squares(rows):
    return pl.pallas_call(
        squares_kernel,
        out_shape=jax.ShapeDtypeStruct((8, 128), F32),
        in_specs=[pl.BlockSpec(memory_space=pltpu.VMEM)],
        out_specs=pl.BlockSpec(memory_space=pltpu.VMEM),
        cost_estimate=pl.CostEstimate(
            flops=50_000_000_000, bytes_accessed=rows.size * 2, transcendentals=0
        ),
        name="squares",
    )(rows)


def per_device(activations, block_ids, enc_weight, enc_bias, dec_weight, dec_bias):
    tok_rows, feature_dim = activations.shape
    active_count = block_ids.shape[1]
    devices = lax.axis_size("lat")
    half = devices // 2
    local_latents = enc_weight.shape[1]
    blocks_dev = local_latents // BLOCK
    nblocks = blocks_dev * devices
    capacity = max(2, 3 * tok_rows * active_count // (2 * nblocks))
    dev_slots = blocks_dev * capacity
    half_slots = half * dev_slots
    halves = [list(range(half)), list(range(half, devices))]

    def exchange(rows, groups=None):
        return lax.all_to_all(
            rows, "lat", split_axis=0, concat_axis=0, axis_index_groups=groups, tiled=True
        )

    def swap(rows, step=half):
        return lax.ppermute(rows, "lat", [(i, i ^ step) for i in range(devices)])

    def pick(select, rows):
        return dot(select, rows, 1, 0).astype(BF16)

    held = swap(activations)
    squares = sum_of_squares(activations)

    flat_ids = block_ids.reshape(-1)
    pairs = flat_ids.shape[0]
    order = jnp.arange(pairs, dtype=jnp.int32)
    same = (flat_ids[:, None] == flat_ids[None, :]) & (order[None, :] < order[:, None])
    slot_of = flat_ids * capacity + jnp.sum(same.astype(jnp.int32), axis=1)
    slot_of = slot_of.reshape(tok_rows, active_count).T
    slot_held = swap(slot_of)
    lower = lax.axis_index("lat") < half
    slots = jnp.arange(2 * half_slots, dtype=jnp.int32)

    def selection(slot, names):
        return jnp.any(names[:, None, None] == slot[None, :, :], axis=1).astype(BF16)

    select = selection(slot_of, slots)
    names = slots[:half_slots] + jnp.where(lower, 0, half_slots)

    got_own = exchange(pick(selection(slot_of, names), activations), halves)
    held, slot_held, got_own, squares = together(held, slot_held, got_own, squares)
    got_held = exchange(pick(selection(slot_held, names), held), halves)

    row_block = (slots[:half_slots] % dev_slots) // capacity
    own = row_block[:, None] == (jnp.arange(local_latents, dtype=jnp.int32) // BLOCK)[None, :]

    def encode(rows):
        output, slopes = activate(dot(rows, enc_weight, 1, 0) + enc_bias[None, :])
        return jnp.where(own, output, 0.0).astype(BF16), jnp.where(own, slopes, 0.0)

    def ordered(own_part, held_part):
        first = jnp.where(lower, own_part, held_part)
        second = jnp.where(lower, held_part, own_part)
        return jnp.concatenate([first, second], axis=0)

    code_own, slope_own = encode(got_own)
    code_held, slope_held = encode(got_held)
    code_rows, slopes = ordered(code_own, code_held), ordered(slope_own, slope_held)

    returned = exchange(dot(code_rows, dec_weight, 1, 0).astype(BF16))
    step = 1
    while step < devices:
        squares = squares + swap(squares, step)
        step *= 2
    returned, squares = together(returned, squares)
    full = dec_bias[None, :] + dot(select, returned, 0, 0)
    errors = (full - activations.astype(F32)).astype(BF16)
    got_errors = exchange(pick(select, errors))

    mean_square = squares[0, 0] / (tok_rows * devices * feature_dim) + 1e-06
    scale = LOSS_SCALE / mean_square
    code_grad = dot(got_errors, dec_weight, 1, 1) * (slopes * scale)
    bias_grad = jnp.sum(code_grad, axis=0)
    code_grad = code_grad.astype(BF16)
    lower_grad, upper_grad = code_grad[:half_slots], code_grad[half_slots:]
    grad_own = jnp.where(lower, lower_grad, upper_grad)
    grad_held = jnp.where(lower, upper_grad, lower_grad)
    enc_grad = (dot(got_own, grad_own, 0, 0) + dot(got_held, grad_held, 0, 0)).astype(BF16)
    dec_grad = (dot(code_rows, got_errors, 0, 0) * scale).astype(BF16)
    return (full.astype(BF16), enc_grad, dec_grad, bias_grad)


def solution(mesh):
    return jax.shard_map(
        per_device,
        mesh=mesh,
        in_specs=(
            P(("grp", "lat"), None),
            P(("grp", "lat"), None),
            P(None, "lat"),
            P("lat"),
            P("lat", None),
            P(),
        ),
        out_specs=(
            P(("grp", "lat"), None),
            P("grp", "lat"),
            P(("grp", "lat"), None),
            P(("grp", "lat")),
        ),
        check_vma=False,
    )
```

```python
import jax
import jax.numpy as jnp
from jax import lax
from jax.experimental import pallas as pl
from jax.experimental.pallas import tpu as pltpu
from jax.sharding import PartitionSpec as P

BLOCK = 64
LOSS_SCALE = 0.5
PIECES = 4
VMEM_LIMIT = 32 * 1024 * 1024
F32 = jnp.float32
BF16 = jnp.bfloat16


def activate(preact):
    inner_arg = 0.7978845608 * (preact + 0.044715 * preact * preact * preact)
    tangent = jnp.tanh(inner_arg)
    output = 0.5 * preact * (1.0 + tangent)
    slopes = 0.5 * (1.0 + tangent) + 0.5 * preact * (1.0 - tangent * tangent) * 0.7978845608 * (
        1.0 + 0.134145 * preact * preact
    )
    return (output, slopes)


def dot(left, right, left_dim, right_dim):
    dims = (((left_dim,), (right_dim,)), ((), ()))
    return lax.dot_general(left, right, dims, preferred_element_type=F32)


def together(*values):
    return lax.optimization_barrier(values)


def squares_kernel(rows_ref, total_ref):
    total = jnp.zeros((8, 128), F32)
    rows, columns = rows_ref.shape
    for i in range(0, columns, 128):
        part = rows_ref[:, i : i + 128].astype(F32)
        total = total + jnp.sum((part * part).reshape(rows // 8, 8, 128), axis=0)
    total_ref[...] = jnp.full((8, 128), jnp.sum(total), F32)


def sum_of_squares(rows):
    return pl.pallas_call(
        squares_kernel,
        out_shape=jax.ShapeDtypeStruct((8, 128), F32),
        in_specs=[pl.BlockSpec(memory_space=pltpu.VMEM)],
        out_specs=pl.BlockSpec(memory_space=pltpu.VMEM),
        cost_estimate=pl.CostEstimate(
            flops=50_000_000_000, bytes_accessed=rows.size * 2, transcendentals=0
        ),
        name="squares",
    )(rows)


def home_kernel(select_ref, select_t_ref, returned_ref, act_ref, bias_ref, full_ref, send_ref):
    full = bias_ref[...] + dot(select_t_ref[...], returned_ref[...], 1, 0)
    full_ref[...] = full.astype(BF16)
    errors = (full - act_ref[...].astype(F32)).astype(BF16)
    send_ref[...] = dot(select_ref[...], errors, 1, 0).astype(BF16)


def rebuild(select, select_t, returned, activations, dec_bias):
    slots, tokens = select.shape
    features = activations.shape[1]
    width = features // PIECES

    def columns(rows):
        return pl.BlockSpec((rows, width), lambda i: (0, i))

    def whole(rows, cols):
        return pl.BlockSpec((rows, cols), lambda i: (0, 0))

    return pl.pallas_call(
        home_kernel,
        grid=(PIECES,),
        out_shape=[
            jax.ShapeDtypeStruct((tokens, features), BF16),
            jax.ShapeDtypeStruct((slots, features), BF16),
        ],
        in_specs=[
            whole(slots, tokens),
            whole(tokens, slots),
            columns(slots),
            columns(tokens),
            columns(1),
        ],
        out_specs=[columns(tokens), columns(slots)],
        cost_estimate=pl.CostEstimate(
            flops=4 * slots * tokens * features,
            bytes_accessed=4 * (slots + tokens) * features,
            transcendentals=0,
        ),
        compiler_params=pltpu.CompilerParams(vmem_limit_bytes=VMEM_LIMIT),
        name="rebuild",
    )(select, select_t, returned, activations, dec_bias)


def grads_kernel(
    count,
    flag_ref,
    squares_ref,
    code_t_ref,
    slopes_ref,
    got_ref,
    dec_ref,
    own_ref,
    held_ref,
    dec_grad_ref,
    enc_grad_ref,
    bias_grad_ref,
    total_ref,
    code_grad_ref,
):
    step = pl.program_id(0)
    scale = LOSS_SCALE / (squares_ref[0:1, 0:1] / count + 1e-06)

    @pl.when(step < PIECES)
    def _():
        got = got_ref[...]
        part = dot(got, dec_ref[...], 1, 1)
        dec_grad_ref[...] = (dot(code_t_ref[...], got, 1, 0) * scale).astype(BF16)

        @pl.when(step == 0)
        def _():
            total_ref[...] = part

        @pl.when(step > 0)
        def _():
            total_ref[...] += part

    @pl.when(step == PIECES - 1)
    def _():
        code_grad = total_ref[...] * (slopes_ref[...] * scale)
        bias_grad_ref[...] = jnp.sum(code_grad, axis=0, keepdims=True)
        code_grad_ref[...] = code_grad.astype(BF16)

    @pl.when(step >= PIECES)
    def _():
        rows = own_ref.shape[0]
        flag = flag_ref[0]
        grad_own = code_grad_ref[pl.ds(pl.multiple_of(flag * rows, rows), rows), :]
        grad_held = code_grad_ref[pl.ds(pl.multiple_of((1 - flag) * rows, rows), rows), :]
        enc_grad = dot(own_ref[...], grad_own, 0, 0) + dot(held_ref[...], grad_held, 0, 0)
        enc_grad_ref[...] = enc_grad.astype(BF16)


def gradients(count, flag, squares, code_t, slopes, got_errors, dec_weight, own_rows, held_rows):
    latents, slots = code_t.shape
    features = dec_weight.shape[1]
    width = features // PIECES
    half_slots = own_rows.shape[0]

    def early(rows):
        return pl.BlockSpec((rows, width), lambda i, _: (0, jnp.minimum(i, PIECES - 1)))

    def late(rows):
        return pl.BlockSpec((rows, width), lambda i, _: (0, jnp.maximum(i - PIECES, 0)))

    def whole(rows, cols):
        return pl.BlockSpec((rows, cols), lambda i, _: (0, 0))

    return pl.pallas_call(
        lambda *refs: grads_kernel(count, *refs),
        grid_spec=pltpu.PrefetchScalarGridSpec(
            num_scalar_prefetch=1,
            grid=(2 * PIECES,),
            in_specs=[
                whole(8, 128),
                whole(latents, slots),
                whole(slots, latents),
                early(slots),
                early(latents),
                late(half_slots),
                late(half_slots),
            ],
            out_specs=[
                early(latents),
                pl.BlockSpec((width, latents), lambda i, _: (jnp.maximum(i - PIECES, 0), 0)),
                whole(1, latents),
            ],
            scratch_shapes=[pltpu.VMEM((slots, latents), F32), pltpu.VMEM((slots, latents), BF16)],
        ),
        out_shape=[
            jax.ShapeDtypeStruct((latents, features), BF16),
            jax.ShapeDtypeStruct((features, latents), BF16),
            jax.ShapeDtypeStruct((1, latents), F32),
        ],
        cost_estimate=pl.CostEstimate(
            flops=6 * slots * latents * features,
            bytes_accessed=2 * features * (2 * slots + 3 * latents),
            transcendentals=0,
        ),
        compiler_params=pltpu.CompilerParams(vmem_limit_bytes=VMEM_LIMIT),
        name="gradients",
    )(flag, squares, code_t, slopes, got_errors, dec_weight, own_rows, held_rows)


def per_device(activations, block_ids, enc_weight, enc_bias, dec_weight, dec_bias):
    tok_rows, feature_dim = activations.shape
    active_count = block_ids.shape[1]
    devices = lax.axis_size("lat")
    half = devices // 2
    local_latents = enc_weight.shape[1]
    blocks_dev = local_latents // BLOCK
    nblocks = blocks_dev * devices
    capacity = max(2, 3 * tok_rows * active_count // (2 * nblocks))
    dev_slots = blocks_dev * capacity
    half_slots = half * dev_slots
    halves = [list(range(half)), list(range(half, devices))]

    def exchange(rows, groups=None):
        return lax.all_to_all(
            rows, "lat", split_axis=0, concat_axis=0, axis_index_groups=groups, tiled=True
        )

    def swap(rows, step=half):
        return lax.ppermute(rows, "lat", [(i, i ^ step) for i in range(devices)])

    def pick(select, rows):
        return dot(select, rows, 1, 0).astype(BF16)

    held = swap(activations)
    squares = sum_of_squares(activations)

    flat_ids = block_ids.reshape(-1)
    pairs = flat_ids.shape[0]
    order = jnp.arange(pairs, dtype=jnp.int32)
    same = (flat_ids[:, None] == flat_ids[None, :]) & (order[None, :] < order[:, None])
    slot_of = flat_ids * capacity + jnp.sum(same.astype(jnp.int32), axis=1)
    slot_of = slot_of.reshape(tok_rows, active_count).T
    slot_held = swap(slot_of)
    lower = lax.axis_index("lat") < half
    slots = jnp.arange(2 * half_slots, dtype=jnp.int32)

    def selection(slot, names):
        return jnp.any(names[:, None, None] == slot[None, :, :], axis=1).astype(BF16)

    select = selection(slot_of, slots)
    select_t = jnp.any(slots[None, :, None] == slot_of.T[:, None, :], axis=2).astype(BF16)
    names = slots[:half_slots] + jnp.where(lower, 0, half_slots)

    got_own = exchange(pick(selection(slot_of, names), activations), halves)
    held, slot_held, got_own, squares = together(held, slot_held, got_own, squares)
    got_held = exchange(pick(selection(slot_held, names), held), halves)

    row_block = (slots[:half_slots] % dev_slots) // capacity
    own = row_block[:, None] == (jnp.arange(local_latents, dtype=jnp.int32) // BLOCK)[None, :]

    def encode(rows):
        output, slopes = activate(dot(rows, enc_weight, 1, 0) + enc_bias[None, :])
        return jnp.where(own, output, 0.0).astype(BF16), jnp.where(own, slopes, 0.0)

    def ordered(own_part, held_part):
        first = jnp.where(lower, own_part, held_part)
        second = jnp.where(lower, held_part, own_part)
        return jnp.concatenate([first, second], axis=0)

    code_own, slope_own = encode(got_own)
    code_held, slope_held = encode(got_held)
    code_rows, slopes = ordered(code_own, code_held), ordered(slope_own, slope_held)

    returned = exchange(dot(code_rows, dec_weight, 1, 0).astype(BF16))
    step = 1
    while step < devices:
        squares = squares + swap(squares, step)
        step *= 2
    returned, squares = together(returned, squares)
    full, send_errors = rebuild(select, select_t, returned, activations, dec_bias[None, :])
    got_errors = exchange(send_errors)
    dec_grad, enc_grad, bias_grad = gradients(
        tok_rows * devices * feature_dim,
        jnp.where(lower, 0, 1).astype(jnp.int32).reshape(1),
        squares,
        code_rows.T,
        slopes,
        got_errors,
        dec_weight,
        got_own,
        got_held,
    )
    return (full, enc_grad, dec_grad, bias_grad.reshape(local_latents))


def solution(mesh):
    return jax.shard_map(
        per_device,
        mesh=mesh,
        in_specs=(
            P(("grp", "lat"), None),
            P(("grp", "lat"), None),
            P(None, "lat"),
            P("lat"),
            P("lat", None),
            P(),
        ),
        out_specs=(
            P(("grp", "lat"), None),
            P("grp", "lat"),
            P(("grp", "lat"), None),
            P(("grp", "lat")),
        ),
        check_vma=False,
    )
```

```python
import jax
import jax.numpy as jnp
from jax import lax
from jax.experimental import pallas as pl
from jax.experimental.pallas import tpu as pltpu
from jax.sharding import PartitionSpec as P

BLOCK = 64
LOSS_SCALE = 0.5
PIECES = 2
COPIES = 4
VMEM_LIMIT = 32 * 1024 * 1024
F32 = jnp.float32
BF16 = jnp.bfloat16


def activate(preact):
    inner_arg = 0.7978845608 * (preact + 0.044715 * preact * preact * preact)
    tangent = jnp.tanh(inner_arg)
    output = 0.5 * preact * (1.0 + tangent)
    slopes = 0.5 * (1.0 + tangent) + 0.5 * preact * (1.0 - tangent * tangent) * 0.7978845608 * (
        1.0 + 0.134145 * preact * preact
    )
    return (output, slopes)


def dot(left, right, left_dim, right_dim):
    dims = (((left_dim,), (right_dim,)), ((), ()))
    return lax.dot_general(left, right, dims, preferred_element_type=F32)


def together(*values):
    return lax.optimization_barrier(values)


def squares_kernel(rows_ref, total_ref):
    total = jnp.zeros((8, 128), F32)
    rows, columns = rows_ref.shape
    for i in range(0, columns, 128):
        part = rows_ref[:, i : i + 128].astype(F32)
        total = total + jnp.sum((part * part).reshape(rows // 8, 8, 128), axis=0)
    total_ref[...] = jnp.full((8, 128), jnp.sum(total), F32)


def sum_of_squares(rows):
    return pl.pallas_call(
        squares_kernel,
        out_shape=jax.ShapeDtypeStruct((8, 128), F32),
        in_specs=[pl.BlockSpec(memory_space=pltpu.VMEM)],
        out_specs=pl.BlockSpec(memory_space=pltpu.VMEM),
        cost_estimate=pl.CostEstimate(
            flops=50_000_000_000, bytes_accessed=rows.size * 2, transcendentals=0
        ),
        name="squares",
    )(rows)


def pass_kernel(value_ref, same_ref):
    same_ref[...] = value_ref[...]


def beside(value):
    return pl.pallas_call(
        pass_kernel,
        out_shape=jax.ShapeDtypeStruct(value.shape, value.dtype),
        in_specs=[pl.BlockSpec(memory_space=pltpu.VMEM)],
        out_specs=pl.BlockSpec(memory_space=pltpu.VMEM),
        cost_estimate=pl.CostEstimate(flops=50_000_000_000, bytes_accessed=8192, transcendentals=0),
        name="beside",
    )(value)


def home_kernel(select_t_ref, returned_ref, far_ref, act_ref, bias_ref, full_ref, errors_ref):
    full = bias_ref[...] + dot(select_t_ref[...], returned_ref[...], 1, 0)
    full = full + far_ref[...].astype(F32)
    full_ref[...] = full.astype(BF16)
    errors = (full - act_ref[...].astype(F32)).astype(BF16)
    errors_ref[...] = errors


def rebuild(select_t, returned, far, activations, dec_bias):
    tokens, slots = select_t.shape
    features = activations.shape[1]
    width = features // PIECES

    def columns(rows):
        return pl.BlockSpec((rows, width), lambda i: (0, i))

    def whole(rows, cols):
        return pl.BlockSpec((rows, cols), lambda i: (0, 0))

    return pl.pallas_call(
        home_kernel,
        grid=(PIECES,),
        out_shape=[
            jax.ShapeDtypeStruct((tokens, features), BF16),
            jax.ShapeDtypeStruct((tokens, features), BF16),
        ],
        in_specs=[
            whole(tokens, slots),
            columns(slots),
            columns(tokens),
            columns(tokens),
            columns(1),
        ],
        out_specs=[columns(tokens), columns(tokens)],
        cost_estimate=pl.CostEstimate(
            flops=2 * slots * tokens * features,
            bytes_accessed=2 * (slots + 4 * tokens) * features,
            transcendentals=0,
        ),
        compiler_params=pltpu.CompilerParams(vmem_limit_bytes=VMEM_LIMIT),
        name="rebuild",
    )(select_t, returned, far, activations, dec_bias)


def grads_kernel(
    count,
    squares_ref,
    code_own_ref,
    code_held_ref,
    slope_own_ref,
    slope_held_ref,
    dec_ref,
    own_ref,
    held_ref,
    got_own_ref,
    got_held_ref,
    dec_grad_ref,
    enc_grad_ref,
    bias_grad_ref,
    dec_out_ref,
    enc_out_ref,
    sems,
):
    scale = LOSS_SCALE / (squares_ref[0:1, 0:1] / count + 1e-06)
    width = dec_ref.shape[1] // COPIES
    copies = []
    grad_own = grad_held = None
    for i in range(COPIES):
        piece = slice(i * width, (i + 1) * width)
        got_own, got_held, dec = got_own_ref[:, piece], got_held_ref[:, piece], dec_ref[:, piece]
        dec_grad = dot(code_own_ref[...], got_own, 1, 0) + dot(code_held_ref[...], got_held, 1, 0)
        dec_out_ref[i] = (dec_grad * scale).astype(BF16)
        copies.append(
            pltpu.make_async_copy(dec_out_ref.at[i], dec_grad_ref.at[:, piece], sems.at[i])
        )
        copies[-1].start()
        part_own, part_held = dot(got_own, dec, 1, 1), dot(got_held, dec, 1, 1)
        grad_own = part_own if i == 0 else grad_own + part_own
        grad_held = part_held if i == 0 else grad_held + part_held
    grad_own = grad_own * (slope_own_ref[...] * scale)
    grad_held = grad_held * (slope_held_ref[...] * scale)
    bias_grad_ref[...] = jnp.sum(grad_own, axis=0, keepdims=True) + jnp.sum(
        grad_held, axis=0, keepdims=True
    )
    grad_own, grad_held = grad_own.astype(BF16), grad_held.astype(BF16)
    for i in range(COPIES):
        piece = slice(i * width, (i + 1) * width)
        enc_grad = dot(own_ref[:, piece], grad_own, 0, 0) + dot(held_ref[:, piece], grad_held, 0, 0)
        enc_out_ref[i] = enc_grad.astype(BF16)
        copies.append(
            pltpu.make_async_copy(enc_out_ref.at[i], enc_grad_ref.at[piece], sems.at[COPIES + i])
        )
        copies[-1].start()
    for copy in copies:
        copy.wait()


def gradients(count, squares, codes, slopes, dec_weight, rows, got):
    latents, features = dec_weight.shape
    slots = got[0].shape[0]
    width = features // COPIES
    vmem = pl.BlockSpec(memory_space=pltpu.VMEM)
    return pl.pallas_call(
        lambda *refs: grads_kernel(count, *refs),
        out_shape=[
            jax.ShapeDtypeStruct((latents, features), BF16),
            jax.ShapeDtypeStruct((features, latents), BF16),
            jax.ShapeDtypeStruct((1, latents), F32),
        ],
        in_specs=[vmem] * 10,
        out_specs=[pl.BlockSpec(memory_space=pl.ANY)] * 2 + [vmem],
        scratch_shapes=[
            pltpu.VMEM((COPIES, latents, width), BF16),
            pltpu.VMEM((COPIES, width, latents), BF16),
            pltpu.SemaphoreType.DMA((2 * COPIES,)),
        ],
        cost_estimate=pl.CostEstimate(
            flops=12 * slots * latents * features,
            bytes_accessed=2 * features * (4 * slots + 3 * latents),
            transcendentals=0,
        ),
        compiler_params=pltpu.CompilerParams(vmem_limit_bytes=VMEM_LIMIT),
        name="gradients",
    )(squares, codes[0].T, codes[1].T, *slopes, dec_weight, *rows, *got)


def per_device(activations, block_ids, enc_weight, enc_bias, dec_weight, dec_bias):
    tok_rows, feature_dim = activations.shape
    active_count = block_ids.shape[1]
    devices = lax.axis_size("lat")
    half = devices // 2
    local_latents = enc_weight.shape[1]
    blocks_dev = local_latents // BLOCK
    nblocks = blocks_dev * devices
    capacity = max(2, 3 * tok_rows * active_count // (2 * nblocks))
    dev_slots = blocks_dev * capacity
    half_slots = half * dev_slots
    halves = [list(range(half)), list(range(half, devices))]

    def swap(rows, step=half):
        return lax.ppermute(rows, "lat", [(i, i ^ step) for i in range(devices)])

    def pick(select, rows):
        return dot(select, rows, 1, 0).astype(BF16)

    def exchange(rows):
        return lax.all_to_all(
            rows, "lat", split_axis=0, concat_axis=0, axis_index_groups=halves, tiled=True
        )

    by_swaps = half <= 8

    def exchange_held(left, right):
        if not by_swaps:
            return exchange(pick(left, right))
        parts = [left[k * dev_slots : (k + 1) * dev_slots] for k in range(half)]
        parts = [pick(part, right) for part in parts]
        return jnp.concatenate(parts[:1] + [swap(parts[k], k) for k in range(1, half)], axis=0)

    steps = [1 << i for i in range((devices - 1).bit_length())]

    def more(squares):
        return squares + swap(squares, steps.pop(0)) if steps else squares

    held = swap(activations)
    squares = sum_of_squares(activations)

    flat_ids = block_ids.reshape(-1)
    pairs = flat_ids.shape[0]
    order = jnp.arange(pairs, dtype=jnp.int32)
    same = (flat_ids[:, None] == flat_ids[None, :]) & (order[None, :] < order[:, None])
    slot_of = flat_ids * capacity + jnp.sum(same.astype(jnp.int32), axis=1)
    slot_of = slot_of.reshape(tok_rows, active_count).T
    slot_held = swap(slot_of)
    me = lax.axis_index("lat")
    slots = jnp.arange(half_slots, dtype=jnp.int32)
    names = slots + (me // half) * half_slots
    names_held = names
    if by_swaps:
        names_held = ((slots // dev_slots) ^ me) * dev_slots + slots % dev_slots

    def selection(slot, names):
        return jnp.any(names[:, None, None] == slot[None, :, :], axis=1).astype(BF16)

    def selection_t(slot, names):
        return jnp.any(names[None, None, :] == slot.T[:, :, None], axis=1).astype(BF16)

    select = selection(slot_of, names)
    got_own = exchange(pick(select, activations))
    held, slot_held, got_own, squares = together(held, slot_held, got_own, squares)
    select_held = selection(slot_held, names_held)
    got_held = exchange_held(select_held, held)
    got_held, squares = together(got_held, more(squares))

    row_block = (slots % dev_slots) // capacity
    own = row_block[:, None] == (jnp.arange(local_latents, dtype=jnp.int32) // BLOCK)[None, :]

    def encode(rows):
        output, slopes = activate(dot(rows, enc_weight, 1, 0) + enc_bias[None, :])
        return jnp.where(own, output, 0.0).astype(BF16), jnp.where(own, slopes, 0.0)

    code_own, slope_own = encode(got_own)
    code_held, slope_held = encode(got_held)

    back_held = exchange_held(code_held, dec_weight)
    back_held, code_own, squares, dec_bias = together(
        back_held, code_own, more(squares), dec_bias[None, :]
    )
    far = swap(pick(selection_t(slot_held, names_held), back_held))
    back_own = exchange(pick(code_own, dec_weight))
    far, back_own, squares, dec_bias = together(far, back_own, more(squares), beside(dec_bias))
    while steps:
        squares = more(squares)
    full, errors = rebuild(selection_t(slot_of, names), back_own, far, activations, dec_bias)

    errors, slope_own = together(errors, slope_own)
    far = swap(errors)
    err_own = exchange(pick(select, errors))
    far, err_own, slope_own = together(far, err_own, beside(slope_own))
    err_held = exchange_held(select_held, far)
    dec_grad, enc_grad, bias_grad = gradients(
        tok_rows * devices * feature_dim,
        squares,
        (code_own, code_held),
        (slope_own, slope_held),
        dec_weight,
        (got_own, got_held),
        (err_own, err_held),
    )
    return (full, enc_grad, dec_grad, bias_grad.reshape(local_latents))


def solution(mesh):
    return jax.shard_map(
        per_device,
        mesh=mesh,
        in_specs=(
            P(("grp", "lat"), None),
            P(("grp", "lat"), None),
            P(None, "lat"),
            P("lat"),
            P("lat", None),
            P(),
        ),
        out_specs=(
            P(("grp", "lat"), None),
            P("grp", "lat"),
            P(("grp", "lat"), None),
            P(("grp", "lat")),
        ),
        check_vma=False,
    )
```

```python
import jax
import jax.numpy as jnp
from jax import lax
from jax.experimental import pallas as pl
from jax.experimental.pallas import tpu as pltpu
from jax.sharding import PartitionSpec as P

BLOCK = 64
LOSS_SCALE = 0.5
PIECES = 4
VMEM_LIMIT = 28 * 1024 * 1024
F32 = jnp.float32
BF16 = jnp.bfloat16


def activate(preact):
    inner_arg = 0.7978845608 * (preact + 0.044715 * preact * preact * preact)
    tangent = jnp.tanh(inner_arg)
    output = 0.5 * preact * (1.0 + tangent)
    slopes = 0.5 * (1.0 + tangent) + 0.5 * preact * (1.0 - tangent * tangent) * 0.7978845608 * (
        1.0 + 0.134145 * preact * preact
    )
    return (output, slopes)


def dot(left, right, left_dim, right_dim):
    dims = (((left_dim,), (right_dim,)), ((), ()))
    return lax.dot_general(left, right, dims, preferred_element_type=F32)


def together(*values):
    return lax.optimization_barrier(values)


def squares_kernel(rows_ref, total_ref):
    total = jnp.zeros((8, 128), F32)
    rows, columns = rows_ref.shape
    for i in range(0, columns, 128):
        part = rows_ref[:, i : i + 128].astype(F32)
        total = total + jnp.sum((part * part).reshape(rows // 8, 8, 128), axis=0)
    total_ref[...] = jnp.full((8, 128), jnp.sum(total), F32)


def sum_of_squares(rows):
    return pl.pallas_call(
        squares_kernel,
        out_shape=jax.ShapeDtypeStruct((8, 128), F32),
        in_specs=[pl.BlockSpec(memory_space=pltpu.VMEM)],
        out_specs=pl.BlockSpec(memory_space=pltpu.VMEM),
        cost_estimate=pl.CostEstimate(
            flops=50_000_000_000, bytes_accessed=rows.size * 2, transcendentals=0
        ),
        name="squares",
    )(rows)


VMEM_SPEC = pl.BlockSpec(memory_space=pltpu.VMEM)
HBM_SPEC = pl.BlockSpec(memory_space=pltpu.HBM)


def columns(ref, i):
    width = ref.shape[1] // PIECES
    return ref.at[:, i * width : (i + 1) * width]


def fetch(source_ref, here_ref, sems):
    copies = [
        pltpu.make_async_copy(columns(source_ref, i), columns(here_ref, i), sems.at[i])
        for i in range(PIECES)
    ]
    for copy in copies:
        copy.start()
    return copies


def store(copies, here_ref, target_ref, sem):
    copies.append(pltpu.make_async_copy(here_ref, target_ref, sem))
    copies[-1].start()


def encode_kernel(
    slot_ref,
    rows_ref,
    enc_ref,
    bias_ref,
    own_ref,
    dec_ref,
    _,
    code_ref,
    slopes_ref,
    partial_ref,
    here_ref,
    out_ref,
    sems,
):
    copies = fetch(rows_ref, here_ref, sems.at[0])
    slots = rows_ref.shape[0]
    width = rows_ref.shape[1] // PIECES
    preact = bias_ref[...]
    for i, copy in enumerate(copies):
        copy.wait()
        preact = preact + dot(
            columns(here_ref, i)[...], enc_ref[i * width : (i + 1) * width, :], 1, 0
        )
    output, slopes = activate(preact)
    own = own_ref[...] > 0
    code = jnp.where(own, output, 0.0).astype(BF16)
    code_ref[...] = code
    slopes_ref[...] = jnp.where(own, slopes, 0.0)
    start = pl.multiple_of(slot_ref[0] * slots, slots)
    target_ref = partial_ref.at[pl.ds(start, slots), :]
    copies = []
    for i in range(PIECES):
        columns(out_ref, i)[...] = dot(code, columns(dec_ref, i)[...], 1, 0).astype(BF16)
        store(copies, columns(out_ref, i), columns(target_ref, i), sems.at[1, i])
    for copy in copies:
        copy.wait()


def encode(place, rows, enc_weight, enc_bias, own, dec_weight, partial_value):
    slots, features = rows.shape
    latents = enc_weight.shape[1]
    return pl.pallas_call(
        encode_kernel,
        out_shape=[
            jax.ShapeDtypeStruct((slots, latents), BF16),
            jax.ShapeDtypeStruct((slots, latents), F32),
            jax.ShapeDtypeStruct((2 * slots, features), BF16),
        ],
        in_specs=[pl.BlockSpec(memory_space=pltpu.SMEM), HBM_SPEC] + [VMEM_SPEC] * 4 + [HBM_SPEC],
        out_specs=[VMEM_SPEC, VMEM_SPEC, HBM_SPEC],
        input_output_aliases={6: 2},
        scratch_shapes=[
            pltpu.VMEM((slots, features), BF16),
            pltpu.VMEM((slots, features), BF16),
            pltpu.SemaphoreType.DMA((2, PIECES)),
        ],
        cost_estimate=pl.CostEstimate(
            flops=4 * slots * latents * features,
            bytes_accessed=4 * features * (slots + latents),
            transcendentals=slots * latents,
        ),
        compiler_params=pltpu.CompilerParams(vmem_limit_bytes=VMEM_LIMIT),
        name="encode",
    )(place, rows, enc_weight, enc_bias, own, dec_weight, partial_value)


def home_kernel(
    select_ref,
    select_t_ref,
    act_ref,
    bias_ref,
    returned_ref,
    full_ref,
    send_ref,
    here_ref,
    full_out_ref,
    send_out_ref,
    sems,
):
    stores = []
    for i, copy in enumerate(fetch(returned_ref, here_ref, sems.at[0])):
        copy.wait()
        full = dot(select_t_ref[...], columns(here_ref, i)[...], 1, 0) + columns(bias_ref, i)[...]
        errors = (full - columns(act_ref, i)[...].astype(F32)).astype(BF16)
        columns(send_out_ref, i)[...] = dot(select_ref[...], errors, 1, 0).astype(BF16)
        store(stores, columns(send_out_ref, i), columns(send_ref, i), sems.at[1, i])
        columns(full_out_ref, i)[...] = full.astype(BF16)
        store(stores, columns(full_out_ref, i), columns(full_ref, i), sems.at[2, i])
    for copy in stores:
        copy.wait()


def rebuild(select, select_t, returned, activations, dec_bias):
    slots, tokens = select.shape
    features = activations.shape[1]
    return pl.pallas_call(
        home_kernel,
        out_shape=[
            pltpu.HBM((tokens, features), BF16),
            pltpu.HBM((slots, features), BF16),
        ],
        in_specs=[VMEM_SPEC] * 4 + [HBM_SPEC],
        out_specs=[HBM_SPEC, HBM_SPEC],
        scratch_shapes=[
            pltpu.VMEM((slots, features), BF16),
            pltpu.VMEM((tokens, features), BF16),
            pltpu.VMEM((slots, features), BF16),
            pltpu.SemaphoreType.DMA((3, PIECES)),
        ],
        cost_estimate=pl.CostEstimate(
            flops=4 * slots * tokens * features,
            bytes_accessed=4 * (slots + tokens) * features,
            transcendentals=0,
        ),
        compiler_params=pltpu.CompilerParams(vmem_limit_bytes=VMEM_LIMIT),
        name="rebuild",
    )(select, select_t, activations, dec_bias, returned)


def grads_kernel(
    count,
    squares_ref,
    code_t_ref,
    slopes_ref,
    dec_t_ref,
    rows_t_ref,
    got_ref,
    dec_grad_ref,
    enc_grad_ref,
    bias_grad_ref,
    here_ref,
    dec_out_ref,
    enc_out_ref,
    sems,
):
    copies = fetch(got_ref, here_ref, sems.at[0])
    scale = LOSS_SCALE / (squares_ref[0:1, 0:1] / count + 1e-06)
    width = got_ref.shape[1] // PIECES
    stores = []
    code_grad = None
    for i, copy in enumerate(copies):
        copy.wait()
        got = columns(here_ref, i)[...]
        columns(dec_out_ref, i)[...] = (dot(code_t_ref[...], got, 1, 0) * scale).astype(BF16)
        store(stores, columns(dec_out_ref, i), columns(dec_grad_ref, i), sems.at[1, i])
        part = dot(got, dec_t_ref[i * width : (i + 1) * width, :], 1, 0)
        code_grad = part if i == 0 else code_grad + part
    code_grad = code_grad * (slopes_ref[...] * scale)
    bias_grad_ref[...] = jnp.sum(code_grad, axis=0, keepdims=True)
    code_grad = code_grad.astype(BF16)
    for i in range(PIECES):
        piece = slice(i * width, (i + 1) * width)
        enc_out_ref[piece, :] = dot(rows_t_ref[piece, :], code_grad, 1, 0).astype(BF16)
        store(stores, enc_out_ref.at[piece], enc_grad_ref.at[piece], sems.at[2, i])
    for copy in stores:
        copy.wait()


def gradients(count, squares, code_t, slopes, dec_t, rows_t, got_errors):
    latents, slots = code_t.shape
    features = dec_t.shape[0]
    return pl.pallas_call(
        lambda *refs: grads_kernel(count, *refs),
        out_shape=[
            jax.ShapeDtypeStruct((latents, features), BF16),
            jax.ShapeDtypeStruct((features, latents), BF16),
            jax.ShapeDtypeStruct((1, latents), F32),
        ],
        in_specs=[VMEM_SPEC] * 5 + [HBM_SPEC],
        out_specs=[HBM_SPEC, HBM_SPEC, VMEM_SPEC],
        scratch_shapes=[
            pltpu.VMEM((slots, features), BF16),
            pltpu.VMEM((latents, features), BF16),
            pltpu.VMEM((features, latents), BF16),
            pltpu.SemaphoreType.DMA((3, PIECES)),
        ],
        cost_estimate=pl.CostEstimate(
            flops=6 * slots * latents * features,
            bytes_accessed=2 * features * (2 * slots + 3 * latents),
            transcendentals=0,
        ),
        compiler_params=pltpu.CompilerParams(vmem_limit_bytes=VMEM_LIMIT),
        name="gradients",
    )(squares, code_t, slopes, dec_t, rows_t, got_errors)


def per_device(activations, block_ids, enc_weight, enc_bias, dec_weight, dec_bias):
    tok_rows, feature_dim = activations.shape
    active_count = block_ids.shape[1]
    devices = lax.axis_size("lat")
    half = devices // 2
    local_latents = enc_weight.shape[1]
    blocks_dev = local_latents // BLOCK
    nblocks = blocks_dev * devices
    capacity = max(2, 3 * tok_rows * active_count // (2 * nblocks))
    dev_slots = blocks_dev * capacity
    half_slots = half * dev_slots
    halves = [list(range(half)), list(range(half, devices))]

    def exchange(rows, groups=None):
        return lax.all_to_all(
            rows, "lat", split_axis=0, concat_axis=0, axis_index_groups=groups, tiled=True
        )

    def swap(rows, step=half):
        return lax.ppermute(rows, "lat", [(i, i ^ step) for i in range(devices)])

    def pick(select, rows):
        return dot(select, rows, 1, 0).astype(BF16)

    held = swap(activations)
    squares = sum_of_squares(activations)

    flat_ids = block_ids.reshape(-1)
    pairs = flat_ids.shape[0]
    order = jnp.arange(pairs, dtype=jnp.int32)
    same = (flat_ids[:, None] == flat_ids[None, :]) & (order[None, :] < order[:, None])
    slot_of = flat_ids * capacity + jnp.sum(same.astype(jnp.int32), axis=1)
    slot_of = slot_of.reshape(tok_rows, active_count).T
    slot_held = swap(slot_of)
    lower = lax.axis_index("lat") < half
    slots = jnp.arange(2 * half_slots, dtype=jnp.int32)

    def selection(slot, names):
        return jnp.any(names[:, None, None] == slot[None, :, :], axis=1).astype(BF16)

    select = selection(slot_of, slots)
    select_t = jnp.any(slots[None, :, None] == slot_of.T[:, None, :], axis=2).astype(BF16)
    names = slots[:half_slots] + jnp.where(lower, 0, half_slots)

    got_own = exchange(pick(selection(slot_of, names), activations), halves)
    held, slot_held, got_own, squares = together(held, slot_held, got_own, squares)
    got_held = exchange(pick(selection(slot_held, names), held), halves)

    row_block = (slots[:half_slots] % dev_slots) // capacity
    own = row_block[:, None] == (jnp.arange(local_latents, dtype=jnp.int32) // BLOCK)[None, :]

    own = own.astype(F32)
    place = jnp.where(lower, 0, 1).astype(jnp.int32).reshape(1)
    bias_row = enc_bias[None, :]
    partial_value = jnp.zeros((2 * half_slots, feature_dim), BF16)
    code_own, slope_own, partial_value = encode(
        place, got_own, enc_weight, bias_row, own, dec_weight, partial_value
    )
    code_held, slope_held, partial_value = encode(
        1 - place, got_held, enc_weight, bias_row, own, dec_weight, partial_value
    )
    returned = exchange(partial_value)

    def ordered(own_part, held_part):
        first = jnp.where(lower, own_part, held_part)
        second = jnp.where(lower, held_part, own_part)
        return jnp.concatenate([first, second], axis=0)

    code_t = ordered(code_own, code_held).T
    slopes = ordered(slope_own, slope_held)
    rows_t = ordered(got_own, got_held).T

    step = 1
    while step < devices:
        squares = squares + swap(squares, step)
        step *= 2
    returned, squares = together(returned, squares)
    full, send_errors = rebuild(select, select_t, returned, activations, dec_bias[None, :])
    got_errors = exchange(send_errors)
    dec_grad, enc_grad, bias_grad = gradients(
        tok_rows * devices * feature_dim, squares, code_t, slopes, dec_weight.T, rows_t, got_errors
    )
    return (full, enc_grad, dec_grad, bias_grad.reshape(local_latents))


def solution(mesh):
    return jax.shard_map(
        per_device,
        mesh=mesh,
        in_specs=(
            P(("grp", "lat"), None),
            P(("grp", "lat"), None),
            P(None, "lat"),
            P("lat"),
            P("lat", None),
            P(),
        ),
        out_specs=(
            P(("grp", "lat"), None),
            P("grp", "lat"),
            P(("grp", "lat"), None),
            P(("grp", "lat")),
        ),
        check_vma=False,
    )
```

```python
import jax
import jax.numpy as jnp
from jax import lax
from jax.experimental import pallas as pl
from jax.experimental.pallas import tpu as pltpu
from jax.sharding import PartitionSpec as P

BLOCK = 64
LOSS_SCALE = 0.5
PIECES = 4
MIB = 1024 * 1024
F32 = jnp.float32
BF16 = jnp.bfloat16


def activate(preact):
    inner_arg = 0.7978845608 * (preact + 0.044715 * preact * preact * preact)
    tangent = jnp.tanh(inner_arg)
    output = 0.5 * preact * (1.0 + tangent)
    slopes = 0.5 * (1.0 + tangent) + 0.5 * preact * (1.0 - tangent * tangent) * 0.7978845608 * (
        1.0 + 0.134145 * preact * preact
    )
    return (output, slopes)


def dot(left, right, left_dim, right_dim):
    dims = (((left_dim,), (right_dim,)), ((), ()))
    return lax.dot_general(left, right, dims, preferred_element_type=F32)


def together(*values):
    return lax.optimization_barrier(values)


def squares_kernel(rows_ref, total_ref):
    total = jnp.zeros((8, 128), F32)
    rows, columns = rows_ref.shape
    for i in range(0, columns, 128):
        part = rows_ref[:, i : i + 128].astype(F32)
        total = total + jnp.sum((part * part).reshape(rows // 8, 8, 128), axis=0)
    total_ref[...] = jnp.full((8, 128), jnp.sum(total), F32)


def sum_of_squares(rows):
    return pl.pallas_call(
        squares_kernel,
        out_shape=jax.ShapeDtypeStruct((8, 128), F32),
        in_specs=[pl.BlockSpec(memory_space=pltpu.VMEM)],
        out_specs=pl.BlockSpec(memory_space=pltpu.VMEM),
        cost_estimate=pl.CostEstimate(
            flops=50_000_000_000, bytes_accessed=rows.size * 2, transcendentals=0
        ),
        name="squares",
    )(rows)


VMEM_SPEC = pl.BlockSpec(memory_space=pltpu.VMEM)
HBM_SPEC = pl.BlockSpec(memory_space=pltpu.HBM)


def columns(ref, i):
    width = ref.shape[1] // PIECES
    return ref.at[:, i * width : (i + 1) * width]


def lines(ref, i):
    height = ref.shape[0] // PIECES
    return ref.at[i * height : (i + 1) * height]


def fetch(*moves):
    copies = []
    for i in range(PIECES):
        copies.append(
            [
                pltpu.make_async_copy(cut(source, i), cut(here, i), sems.at[i])
                for cut, source, here, sems in moves
            ]
        )
        for copy in copies[-1]:
            copy.start()
    return copies


def finish(copies):
    for copy in copies:
        copy.wait()


def store(copies, here_ref, target_ref, sem):
    copies.append(pltpu.make_async_copy(here_ref, target_ref, sem))
    copies[-1].start()


def encode_kernel(
    dev_slots,
    capacity,
    slot_ref,
    bias_ref,
    rows_ref,
    enc_ref,
    dec_ref,
    _,
    code_ref,
    slopes_ref,
    partial_ref,
    rows_here,
    enc_here,
    dec_here,
    code_here,
    slopes_here,
    out_here,
    sems,
):
    slots, latents = slopes_here.shape
    copies = fetch(
        (columns, rows_ref, rows_here, sems.at[0]),
        (lines, enc_ref, enc_here, sems.at[1]),
    )
    dec_copies = fetch((columns, dec_ref, dec_here, sems.at[2]))
    preact = bias_ref[...]
    for i in range(PIECES):
        finish(copies[i])
        preact = preact + dot(columns(rows_here, i)[...], lines(enc_here, i)[...], 1, 0)
    output, slopes = activate(preact)
    row = lax.broadcasted_iota(jnp.int32, (slots, latents), 0)
    latent = lax.broadcasted_iota(jnp.int32, (slots, latents), 1)
    own = lax.div(lax.rem(row, dev_slots), capacity) == lax.div(latent, BLOCK)
    code = jnp.where(own, output, 0.0).astype(BF16)
    stores = []
    code_here[...] = code
    store(stores, code_here, code_ref, sems.at[3, 0])
    slopes_here[...] = jnp.where(own, slopes, 0.0)
    store(stores, slopes_here, slopes_ref, sems.at[3, 1])
    start = pl.multiple_of(slot_ref[0] * slots, slots)
    target_ref = partial_ref.at[pl.ds(start, slots), :]
    for i in range(PIECES):
        finish(dec_copies[i])
        columns(out_here, i)[...] = dot(code, columns(dec_here, i)[...], 1, 0).astype(BF16)
        store(stores, columns(out_here, i), columns(target_ref, i), sems.at[4, i])
    finish(stores)


def encode(dev_slots, capacity, place, rows, enc_weight, enc_bias, dec_weight, partial_value):
    slots, features = rows.shape
    latents = enc_weight.shape[1]
    return pl.pallas_call(
        lambda *refs: encode_kernel(dev_slots, capacity, *refs),
        out_shape=[
            pltpu.HBM((slots, latents), BF16),
            pltpu.HBM((slots, latents), F32),
            pltpu.HBM((2 * slots, features), BF16),
        ],
        in_specs=[pl.BlockSpec(memory_space=pltpu.SMEM), VMEM_SPEC] + [HBM_SPEC] * 4,
        out_specs=[HBM_SPEC] * 3,
        input_output_aliases={5: 2},
        scratch_shapes=[
            pltpu.VMEM((slots, features), BF16),
            pltpu.VMEM((features, latents), BF16),
            pltpu.VMEM((latents, features), BF16),
            pltpu.VMEM((slots, latents), BF16),
            pltpu.VMEM((slots, latents), F32),
            pltpu.VMEM((slots, features), BF16),
            pltpu.SemaphoreType.DMA((5, PIECES)),
        ],
        cost_estimate=pl.CostEstimate(
            flops=4 * slots * latents * features,
            bytes_accessed=4 * features * (slots + latents),
            transcendentals=slots * latents,
        ),
        compiler_params=pltpu.CompilerParams(vmem_limit_bytes=62 * MIB),
        name="encode",
    )(place, enc_bias, rows, enc_weight, dec_weight, partial_value)


def home_kernel(
    select_ref,
    select_t_ref,
    bias_ref,
    act_ref,
    returned_ref,
    full_ref,
    send_ref,
    act_here,
    here_ref,
    full_out_ref,
    send_out_ref,
    sems,
):
    moves = fetch(
        (columns, returned_ref, here_ref, sems.at[0]), (columns, act_ref, act_here, sems.at[3])
    )
    stores = []
    for i, copies in enumerate(moves):
        finish(copies)
        full = dot(select_t_ref[...], columns(here_ref, i)[...], 1, 0) + columns(bias_ref, i)[...]
        errors = (full - columns(act_here, i)[...].astype(F32)).astype(BF16)
        columns(send_out_ref, i)[...] = dot(select_ref[...], errors, 1, 0).astype(BF16)
        store(stores, columns(send_out_ref, i), columns(send_ref, i), sems.at[1, i])
        columns(full_out_ref, i)[...] = full.astype(BF16)
        store(stores, columns(full_out_ref, i), columns(full_ref, i), sems.at[2, i])
    finish(stores)


def rebuild(select, select_t, returned, activations, dec_bias):
    slots, tokens = select.shape
    features = activations.shape[1]
    return pl.pallas_call(
        home_kernel,
        out_shape=[
            pltpu.HBM((tokens, features), BF16),
            pltpu.HBM((slots, features), BF16),
        ],
        in_specs=[VMEM_SPEC] * 3 + [HBM_SPEC] * 2,
        out_specs=[HBM_SPEC, HBM_SPEC],
        scratch_shapes=[
            pltpu.VMEM((tokens, features), BF16),
            pltpu.VMEM((slots, features), BF16),
            pltpu.VMEM((tokens, features), BF16),
            pltpu.VMEM((slots, features), BF16),
            pltpu.SemaphoreType.DMA((4, PIECES)),
        ],
        cost_estimate=pl.CostEstimate(
            flops=4 * slots * tokens * features,
            bytes_accessed=4 * (slots + tokens) * features,
            transcendentals=0,
        ),
        compiler_params=pltpu.CompilerParams(vmem_limit_bytes=48 * MIB),
        name="rebuild",
    )(select, select_t, dec_bias, activations, returned)


def grads_kernel(
    count,
    squares_ref,
    code_t_ref,
    slopes_ref,
    dec_t_ref,
    rows_t_ref,
    got_ref,
    dec_grad_ref,
    enc_grad_ref,
    bias_grad_ref,
    code_t_here,
    slopes_here,
    dec_t_here,
    rows_t_here,
    got_here,
    dec_out,
    enc_out,
    sems,
):
    first = []
    store(first, code_t_ref, code_t_here, sems.at[5, 0])
    copies = fetch(
        (columns, got_ref, got_here, sems.at[0]),
        (lines, dec_t_ref, dec_t_here, sems.at[1]),
    )
    second = []
    store(second, slopes_ref, slopes_here, sems.at[5, 1])
    rows_copies = fetch((lines, rows_t_ref, rows_t_here, sems.at[2]))
    scale = LOSS_SCALE / (squares_ref[0:1, 0:1] / count + 1e-06)
    finish(first)
    stores = []
    code_grad = None
    for i in range(PIECES):
        finish(copies[i])
        got = columns(got_here, i)[...]
        columns(dec_out, i)[...] = (dot(code_t_here[...], got, 1, 0) * scale).astype(BF16)
        store(stores, columns(dec_out, i), columns(dec_grad_ref, i), sems.at[3, i])
        part = dot(got, lines(dec_t_here, i)[...], 1, 0)
        code_grad = part if i == 0 else code_grad + part
    finish(second)
    code_grad = code_grad * (slopes_here[...] * scale)
    bias_grad_ref[...] = jnp.sum(code_grad, axis=0, keepdims=True)
    code_grad = code_grad.astype(BF16)
    for i in range(PIECES):
        finish(rows_copies[i])
        lines(enc_out, i)[...] = dot(lines(rows_t_here, i)[...], code_grad, 1, 0).astype(BF16)
        store(stores, lines(enc_out, i), lines(enc_grad_ref, i), sems.at[4, i])
    finish(stores)


def gradients(count, squares, code_t, slopes, dec_t, rows_t, got_errors):
    latents, slots = code_t.shape
    features = dec_t.shape[0]
    return pl.pallas_call(
        lambda *refs: grads_kernel(count, *refs),
        out_shape=[
            pltpu.HBM((latents, features), BF16),
            pltpu.HBM((features, latents), BF16),
            jax.ShapeDtypeStruct((1, latents), F32),
        ],
        in_specs=[VMEM_SPEC] + [HBM_SPEC] * 5,
        out_specs=[HBM_SPEC, HBM_SPEC, VMEM_SPEC],
        scratch_shapes=[
            pltpu.VMEM((latents, slots), BF16),
            pltpu.VMEM((slots, latents), F32),
            pltpu.VMEM((features, latents), BF16),
            pltpu.VMEM((features, slots), BF16),
            pltpu.VMEM((slots, features), BF16),
            pltpu.VMEM((latents, features), BF16),
            pltpu.VMEM((features, latents), BF16),
            pltpu.SemaphoreType.DMA((6, PIECES)),
        ],
        cost_estimate=pl.CostEstimate(
            flops=6 * slots * latents * features,
            bytes_accessed=2 * features * (2 * slots + 3 * latents),
            transcendentals=0,
        ),
        compiler_params=pltpu.CompilerParams(vmem_limit_bytes=60 * MIB),
        name="gradients",
    )(squares, code_t, slopes, dec_t, rows_t, got_errors)


def per_device(activations, block_ids, enc_weight, enc_bias, dec_weight, dec_bias):
    tok_rows, feature_dim = activations.shape
    active_count = block_ids.shape[1]
    devices = lax.axis_size("lat")
    half = devices // 2
    local_latents = enc_weight.shape[1]
    blocks_dev = local_latents // BLOCK
    nblocks = blocks_dev * devices
    capacity = max(2, 3 * tok_rows * active_count // (2 * nblocks))
    dev_slots = blocks_dev * capacity
    half_slots = half * dev_slots
    halves = [list(range(half)), list(range(half, devices))]

    def exchange(rows, groups=None):
        return lax.all_to_all(
            rows, "lat", split_axis=0, concat_axis=0, axis_index_groups=groups, tiled=True
        )

    def swap(rows, step=half):
        return lax.ppermute(rows, "lat", [(i, i ^ step) for i in range(devices)])

    def pick(select, rows):
        return dot(select, rows, 1, 0).astype(BF16)

    held = swap(activations)
    squares = sum_of_squares(activations)

    ids = block_ids.T
    order = jnp.arange(tok_rows, dtype=jnp.int32)
    same = jnp.any(ids[:, :, None, None] == ids.T[None, None, :, :], axis=3)
    same = same & (order[None, None, :] < order[None, :, None])
    slot_of = ids * capacity + jnp.sum(same.astype(jnp.int32), axis=2)
    slot_held = swap(slot_of)
    lower = lax.axis_index("lat") < half
    slots = jnp.arange(2 * half_slots, dtype=jnp.int32)

    def selection(slot, names):
        return jnp.any(names[:, None, None] == slot[None, :, :], axis=1).astype(BF16)

    select = selection(slot_of, slots)
    select_t = jnp.any(slots[None, :, None] == slot_of.T[:, None, :], axis=2).astype(BF16)
    names = slots[:half_slots] + jnp.where(lower, 0, half_slots)

    got_own = exchange(pick(selection(slot_of, names), activations), halves)
    held, slot_held, got_own, squares = together(held, slot_held, got_own, squares)
    got_held = exchange(pick(selection(slot_held, names), held), halves)
    step = 1
    while step < min(4, devices):
        squares = squares + swap(squares, step)
        step *= 2
    got_held, squares = together(got_held, squares)

    place = jnp.where(lower, 0, 1).astype(jnp.int32).reshape(1)
    bias_row = enc_bias[None, :]
    partial_value = jnp.zeros((2 * half_slots, feature_dim), BF16)
    code_own, slope_own, partial_value = encode(
        dev_slots, capacity, place, got_own, enc_weight, bias_row, dec_weight, partial_value
    )
    code_held, slope_held, partial_value = encode(
        dev_slots, capacity, 1 - place, got_held, enc_weight, bias_row, dec_weight, partial_value
    )
    returned = exchange(partial_value)

    def ordered(own_part, held_part):
        first = jnp.where(lower, own_part, held_part)
        second = jnp.where(lower, held_part, own_part)
        return jnp.concatenate([first, second], axis=0)

    code_t = ordered(code_own, code_held).T
    slopes = ordered(slope_own, slope_held)
    rows_t = ordered(got_own, got_held).T

    while step < devices:
        squares = squares + swap(squares, step)
        step *= 2
    returned, squares = together(returned, squares)
    full, send_errors = rebuild(select, select_t, returned, activations, dec_bias[None, :])
    got_errors = exchange(send_errors)
    dec_grad, enc_grad, bias_grad = gradients(
        tok_rows * devices * feature_dim, squares, code_t, slopes, dec_weight.T, rows_t, got_errors
    )
    return (full, enc_grad, dec_grad, bias_grad.reshape(local_latents))


def solution(mesh):
    return jax.shard_map(
        per_device,
        mesh=mesh,
        in_specs=(
            P(("grp", "lat"), None),
            P(("grp", "lat"), None),
            P(None, "lat"),
            P("lat"),
            P("lat", None),
            P(),
        ),
        out_specs=(
            P(("grp", "lat"), None),
            P("grp", "lat"),
            P(("grp", "lat"), None),
            P(("grp", "lat")),
        ),
        check_vma=False,
    )
```

```python
import jax
import jax.numpy as jnp
from jax import lax
from jax.experimental import pallas as pl
from jax.experimental.pallas import tpu as pltpu
from jax.sharding import PartitionSpec as P

BLOCK = 64
LOSS_SCALE = 0.5
PIECES = 4
MIB = 1024 * 1024
F32 = jnp.float32
BF16 = jnp.bfloat16


def activate(preact):
    inner_arg = 0.7978845608 * (preact + 0.044715 * preact * preact * preact)
    tangent = jnp.tanh(inner_arg)
    output = 0.5 * preact * (1.0 + tangent)
    slopes = 0.5 * (1.0 + tangent) + 0.5 * preact * (1.0 - tangent * tangent) * 0.7978845608 * (
        1.0 + 0.134145 * preact * preact
    )
    return (output, slopes)


def dot(left, right, left_dim, right_dim):
    dims = (((left_dim,), (right_dim,)), ((), ()))
    return lax.dot_general(left, right, dims, preferred_element_type=F32)


def together(*values):
    return lax.optimization_barrier(values)


def squares_kernel(rows_ref, total_ref):
    total = jnp.zeros((8, 128), F32)
    rows, columns = rows_ref.shape
    for i in range(0, columns, 128):
        part = rows_ref[:, i : i + 128].astype(F32)
        total = total + jnp.sum((part * part).reshape(rows // 8, 8, 128), axis=0)
    total_ref[...] = jnp.full((8, 128), jnp.sum(total), F32)


def pass_kernel(value_ref, same_ref):
    same_ref[...] = value_ref[...]


def beside(value):
    return pl.pallas_call(
        pass_kernel,
        out_shape=jax.ShapeDtypeStruct(value.shape, value.dtype),
        in_specs=[VMEM_SPEC],
        out_specs=VMEM_SPEC,
        cost_estimate=pl.CostEstimate(flops=50_000_000_000, bytes_accessed=8192, transcendentals=0),
        name="beside",
    )(value)


def sum_of_squares(rows):
    return pl.pallas_call(
        squares_kernel,
        out_shape=jax.ShapeDtypeStruct((8, 128), F32),
        in_specs=[pl.BlockSpec(memory_space=pltpu.VMEM)],
        out_specs=pl.BlockSpec(memory_space=pltpu.VMEM),
        cost_estimate=pl.CostEstimate(
            flops=50_000_000_000, bytes_accessed=rows.size * 2, transcendentals=0
        ),
        name="squares",
    )(rows)


VMEM_SPEC = pl.BlockSpec(memory_space=pltpu.VMEM)
HBM_SPEC = pl.BlockSpec(memory_space=pltpu.HBM)


def columns(ref, i):
    width = ref.shape[1] // PIECES
    return ref.at[:, i * width : (i + 1) * width]


def lines(ref, i):
    height = ref.shape[0] // PIECES
    return ref.at[i * height : (i + 1) * height]


def two_parts(refs, i):
    first, second = refs
    width = 2 * first.shape[1] // PIECES
    ref = first if i < PIECES // 2 else second
    i = i % (PIECES // 2)
    return ref.at[:, i * width : (i + 1) * width]


def fetch(*moves):
    copies = []
    for i in range(PIECES):
        copies.append(
            [
                pltpu.make_async_copy(
                    two_parts(source, i) if isinstance(source, tuple) else cut(source, i),
                    cut(here, i),
                    sems.at[i],
                )
                for cut, source, here, sems in moves
            ]
        )
        for copy in copies[-1]:
            copy.start()
    return copies


def finish(copies):
    for copy in copies:
        copy.wait()


def store(copies, here_ref, target_ref, sem):
    copies.append(pltpu.make_async_copy(here_ref, target_ref, sem))
    copies[-1].start()


def encode_kernel(
    dev_slots,
    capacity,
    bias_ref,
    rows_f_ref,
    rows_g_ref,
    enc_ref,
    dec_ref,
    code_ref,
    slopes_ref,
    partial_ref,
    rows_here,
    enc_here,
    dec_here,
    code_here,
    slopes_here,
    out_here,
    sems,
):
    slots, latents = slopes_here.shape
    copies = fetch(
        (columns, (rows_f_ref, rows_g_ref), rows_here, sems.at[0]),
        (lines, enc_ref, enc_here, sems.at[1]),
    )
    dec_copies = fetch((columns, dec_ref, dec_here, sems.at[2]))
    preact = bias_ref[...]
    for i in range(PIECES):
        finish(copies[i])
        preact = preact + dot(columns(rows_here, i)[...], lines(enc_here, i)[...], 1, 0)
    output, slopes = activate(preact)
    row = lax.broadcasted_iota(jnp.int32, (slots, latents), 0)
    latent = lax.broadcasted_iota(jnp.int32, (slots, latents), 1)
    own = lax.div(lax.rem(row, dev_slots), capacity) == lax.div(latent, BLOCK)
    code = jnp.where(own, output, 0.0).astype(BF16)
    stores = []
    code_here[...] = code
    store(stores, code_here, code_ref, sems.at[3, 0])
    slopes_here[...] = jnp.where(own, slopes, 0.0)
    store(stores, slopes_here, slopes_ref, sems.at[3, 1])
    for i in range(PIECES):
        finish(dec_copies[i])
        columns(out_here, i)[...] = dot(code, columns(dec_here, i)[...], 1, 0).astype(BF16)
        store(stores, columns(out_here, i), columns(partial_ref, i), sems.at[4, i])
    finish(stores)


def encode(dev_slots, capacity, rows, enc_weight, enc_bias, dec_weight):
    slots = rows[0].shape[0]
    features, latents = enc_weight.shape
    return pl.pallas_call(
        lambda *refs: encode_kernel(dev_slots, capacity, *refs),
        out_shape=[
            pltpu.HBM((slots, latents), BF16),
            pltpu.HBM((slots, latents), F32),
            pltpu.HBM((slots, features), BF16),
        ],
        in_specs=[VMEM_SPEC] + [HBM_SPEC] * 4,
        out_specs=[HBM_SPEC] * 3,
        scratch_shapes=[
            pltpu.VMEM((slots, features), BF16),
            pltpu.VMEM((features, latents), BF16),
            pltpu.VMEM((latents, features), BF16),
            pltpu.VMEM((slots, latents), BF16),
            pltpu.VMEM((slots, latents), F32),
            pltpu.VMEM((slots, features), BF16),
            pltpu.SemaphoreType.DMA((5, PIECES)),
        ],
        cost_estimate=pl.CostEstimate(
            flops=4 * slots * latents * features,
            bytes_accessed=4 * features * (slots + latents),
            transcendentals=slots * latents,
        ),
        compiler_params=pltpu.CompilerParams(vmem_limit_bytes=62 * MIB),
        name="encode",
    )(enc_bias, *rows, enc_weight, dec_weight)


def home_kernel(
    select_ref,
    select_t_ref,
    bias_ref,
    act_ref,
    returned_ref,
    full_ref,
    errors_ref,
    send_ref,
    act_here,
    here_ref,
    full_out_ref,
    errors_out_ref,
    send_out_ref,
    sems,
):
    moves = fetch(
        (columns, returned_ref, here_ref, sems.at[0]), (columns, act_ref, act_here, sems.at[3])
    )
    stores = []
    for i, copies in enumerate(moves):
        finish(copies)
        full = dot(select_t_ref[...], columns(here_ref, i)[...], 1, 0) + columns(bias_ref, i)[...]
        errors = (full - columns(act_here, i)[...].astype(F32)).astype(BF16)
        if i < PIECES // 2:
            columns(errors_out_ref, i)[...] = errors
            out, target = columns(errors_out_ref, i), two_parts((errors_ref, send_ref), i)
        else:
            columns(send_out_ref, i)[...] = dot(select_ref[...], errors, 1, 0).astype(BF16)
            out, target = columns(send_out_ref, i), two_parts((errors_ref, send_ref), i)
        store(stores, out, target, sems.at[1, i])
        columns(full_out_ref, i)[...] = full.astype(BF16)
        store(stores, columns(full_out_ref, i), columns(full_ref, i), sems.at[2, i])
    finish(stores)


def rebuild(select, select_t, returned, activations, dec_bias):
    slots, tokens = select.shape
    features = activations.shape[1]
    return pl.pallas_call(
        home_kernel,
        out_shape=[
            pltpu.HBM((tokens, features), BF16),
            pltpu.HBM((tokens, features // 2), BF16),
            pltpu.HBM((slots, features // 2), BF16),
        ],
        in_specs=[VMEM_SPEC] * 3 + [HBM_SPEC] * 2,
        out_specs=[HBM_SPEC] * 3,
        scratch_shapes=[
            pltpu.VMEM((tokens, features), BF16),
            pltpu.VMEM((slots, features), BF16),
            pltpu.VMEM((tokens, features), BF16),
            pltpu.VMEM((tokens, features), BF16),
            pltpu.VMEM((slots, features), BF16),
            pltpu.SemaphoreType.DMA((4, PIECES)),
        ],
        cost_estimate=pl.CostEstimate(
            flops=4 * slots * tokens * features,
            bytes_accessed=4 * (slots + tokens) * features,
            transcendentals=0,
        ),
        compiler_params=pltpu.CompilerParams(vmem_limit_bytes=48 * MIB),
        name="rebuild",
    )(select, select_t, dec_bias, activations, returned)


def grads_kernel(
    count,
    squares_ref,
    code_t_ref,
    slopes_ref,
    dec_t_ref,
    rows_t_ref,
    got_f_ref,
    got_g_ref,
    dec_grad_ref,
    enc_grad_ref,
    bias_grad_ref,
    code_t_here,
    slopes_here,
    dec_t_here,
    rows_t_here,
    got_here,
    dec_out,
    enc_out,
    sems,
):
    first = []
    store(first, code_t_ref, code_t_here, sems.at[5, 0])
    copies = fetch(
        (columns, (got_f_ref, got_g_ref), got_here, sems.at[0]),
        (lines, dec_t_ref, dec_t_here, sems.at[1]),
    )
    second = []
    store(second, slopes_ref, slopes_here, sems.at[5, 1])
    scale = LOSS_SCALE / (squares_ref[0:1, 0:1] / count + 1e-06)
    finish(first)
    stores = []
    code_grad = None
    for i in range(PIECES):
        finish(copies[i])
        if i == 1:
            rows_copies = fetch((lines, rows_t_ref, rows_t_here, sems.at[2]))
        got = columns(got_here, i)[...]
        columns(dec_out, i)[...] = (dot(code_t_here[...], got, 1, 0) * scale).astype(BF16)
        store(stores, columns(dec_out, i), columns(dec_grad_ref, i), sems.at[3, i])
        part = dot(got, lines(dec_t_here, i)[...], 1, 0)
        code_grad = part if i == 0 else code_grad + part
    finish(second)
    code_grad = code_grad * (slopes_here[...] * scale)
    bias_grad_ref[...] = jnp.sum(code_grad, axis=0, keepdims=True)
    code_grad = code_grad.astype(BF16)
    for i in range(PIECES):
        finish(rows_copies[i])
        lines(enc_out, i)[...] = dot(lines(rows_t_here, i)[...], code_grad, 1, 0).astype(BF16)
        store(stores, lines(enc_out, i), lines(enc_grad_ref, i), sems.at[4, i])
    finish(stores)


def gradients(count, squares, code_t, slopes, dec_t, rows_t, got_errors):
    latents, slots = code_t.shape
    features = dec_t.shape[0]
    return pl.pallas_call(
        lambda *refs: grads_kernel(count, *refs),
        out_shape=[
            pltpu.HBM((latents, features), BF16),
            pltpu.HBM((features, latents), BF16),
            jax.ShapeDtypeStruct((1, latents), F32),
        ],
        in_specs=[VMEM_SPEC] + [HBM_SPEC] * 6,
        out_specs=[HBM_SPEC, HBM_SPEC, VMEM_SPEC],
        scratch_shapes=[
            pltpu.VMEM((latents, slots), BF16),
            pltpu.VMEM((slots, latents), F32),
            pltpu.VMEM((features, latents), BF16),
            pltpu.VMEM((features, slots), BF16),
            pltpu.VMEM((slots, features), BF16),
            pltpu.VMEM((latents, features), BF16),
            pltpu.VMEM((features, latents), BF16),
            pltpu.SemaphoreType.DMA((6, PIECES)),
        ],
        cost_estimate=pl.CostEstimate(
            flops=6 * slots * latents * features,
            bytes_accessed=2 * features * (2 * slots + 3 * latents),
            transcendentals=0,
        ),
        compiler_params=pltpu.CompilerParams(vmem_limit_bytes=60 * MIB),
        name="gradients",
    )(squares, code_t, slopes, dec_t, rows_t, *got_errors)


def per_device(activations, block_ids, enc_weight, enc_bias, dec_weight, dec_bias):
    tok_rows, feature_dim = activations.shape
    active_count = block_ids.shape[1]
    devices = lax.axis_size("lat")
    half = devices // 2
    local_latents = enc_weight.shape[1]
    blocks_dev = local_latents // BLOCK
    nblocks = blocks_dev * devices
    capacity = max(2, 3 * tok_rows * active_count // (2 * nblocks))
    dev_slots = blocks_dev * capacity
    half_slots = half * dev_slots
    side = feature_dim // 2

    def exchange(rows):
        return lax.all_to_all(rows, "lat", split_axis=0, concat_axis=0, tiled=True)

    def swap(rows, step=half):
        return lax.ppermute(rows, "lat", [(i, i ^ step) for i in range(devices)])

    def pick(select, rows):
        return dot(select, rows, 1, 0).astype(BF16)

    ids = block_ids.T
    order = jnp.arange(tok_rows, dtype=jnp.int32)
    same = jnp.any(ids[:, :, None, None] == ids.T[None, None, :, :], axis=3)
    same = same & (order[None, None, :] < order[None, :, None])
    slot_of = ids * capacity + jnp.sum(same.astype(jnp.int32), axis=2)
    slot_held = swap(slot_of)
    me = lax.axis_index("lat")
    slots = jnp.arange(2 * half_slots, dtype=jnp.int32)
    crossed = ((slots // dev_slots) ^ me) * dev_slots + slots % dev_slots

    def selection(slot, names):
        return jnp.any(names[:, None, None] == slot[None, :, :], axis=1).astype(BF16)

    select = selection(slot_of, slots)
    select_t = jnp.any(slots[None, None, :] == slot_of.T[:, :, None], axis=1).astype(BF16)
    select_own = selection(slot_of, crossed[:half_slots])
    select_held = selection(slot_held, crossed[:half_slots])
    by_swaps = half <= 8

    def deliver(tokens, by_slot, value):
        got = exchange(by_slot)
        if not by_swaps:
            return exchange(pick(select, tokens)), got, value
        held, value = together(swap(tokens), value)
        rows = jnp.zeros((devices, dev_slots, tokens.shape[1]), BF16)
        for choice, source, other in ((select_own, tokens, 0), (select_held, held, half)):
            for k in range(half):
                part = pick(choice[k * dev_slots : (k + 1) * dev_slots], source)
                part = swap(part, k) if k else part
                rows = lax.dynamic_update_index_in_dim(rows, part, me ^ (k + other), 0)
        return rows.reshape(devices * dev_slots, tokens.shape[1]), got, value

    act_f, act_g = activations[:, :side], activations[:, side:]
    rows_f, rows_g, squares = deliver(act_f, pick(select, act_g), sum_of_squares(activations))

    code_rows, slopes, partial_value = encode(
        dev_slots, capacity, (rows_f, rows_g), enc_weight, enc_bias[None, :], dec_weight
    )
    returned = exchange(partial_value)
    code_t = code_rows.T
    rows_t = jnp.concatenate([rows_f.T, rows_g.T], axis=0)

    step = 1
    while step < devices:
        squares = squares + swap(squares, step)
        step *= 2
    returned, squares = together(returned, squares)
    full, err_f, send_g = rebuild(select, select_t, returned, activations, dec_bias[None, :])
    got_f, got_g, squares = deliver(err_f, send_g, beside(squares))
    dec_grad, enc_grad, bias_grad = gradients(
        tok_rows * devices * feature_dim,
        squares,
        code_t,
        slopes,
        dec_weight.T,
        rows_t,
        (got_f, got_g),
    )
    return (full, enc_grad, dec_grad, bias_grad.reshape(local_latents))


def solution(mesh):
    return jax.shard_map(
        per_device,
        mesh=mesh,
        in_specs=(
            P(("grp", "lat"), None),
            P(("grp", "lat"), None),
            P(None, "lat"),
            P("lat"),
            P("lat", None),
            P(),
        ),
        out_specs=(
            P(("grp", "lat"), None),
            P("grp", "lat"),
            P(("grp", "lat"), None),
            P(("grp", "lat")),
        ),
        check_vma=False,
    )
```

```python
import jax
import jax.numpy as jnp
from jax import lax
from jax.experimental import pallas as pl
from jax.experimental.pallas import tpu as pltpu
from jax.sharding import PartitionSpec as P

BLOCK = 64
LOSS_SCALE = 0.5
PIECES = 4
MIB = 1024 * 1024
F32 = jnp.float32
BF16 = jnp.bfloat16


def activate(preact):
    inner_arg = 0.7978845608 * (preact + 0.044715 * preact * preact * preact)
    tangent = jnp.tanh(inner_arg)
    output = 0.5 * preact * (1.0 + tangent)
    slopes = 0.5 * (1.0 + tangent) + 0.5 * preact * (1.0 - tangent * tangent) * 0.7978845608 * (
        1.0 + 0.134145 * preact * preact
    )
    return (output, slopes)


def dot(left, right, left_dim, right_dim):
    dims = (((left_dim,), (right_dim,)), ((), ()))
    return lax.dot_general(left, right, dims, preferred_element_type=F32)


def together(*values):
    return lax.optimization_barrier(values)


def squares_kernel(rows_ref, total_ref):
    total = jnp.zeros((8, 128), F32)
    rows, columns = rows_ref.shape
    for i in range(0, columns, 128):
        part = rows_ref[:, i : i + 128].astype(F32)
        total = total + jnp.sum((part * part).reshape(rows // 8, 8, 128), axis=0)
    total_ref[...] = jnp.full((8, 128), jnp.sum(total), F32)


def pass_kernel(value_ref, same_ref):
    same_ref[...] = value_ref[...]


def beside(value):
    return pl.pallas_call(
        pass_kernel,
        out_shape=jax.ShapeDtypeStruct(value.shape, value.dtype),
        in_specs=[VMEM_SPEC],
        out_specs=VMEM_SPEC,
        cost_estimate=pl.CostEstimate(flops=50_000_000_000, bytes_accessed=8192, transcendentals=0),
        name="beside",
    )(value)


def sum_of_squares(rows):
    return pl.pallas_call(
        squares_kernel,
        out_shape=jax.ShapeDtypeStruct((8, 128), F32),
        in_specs=[pl.BlockSpec(memory_space=pltpu.VMEM)],
        out_specs=pl.BlockSpec(memory_space=pltpu.VMEM),
        cost_estimate=pl.CostEstimate(
            flops=50_000_000_000, bytes_accessed=rows.size * 2, transcendentals=0
        ),
        name="squares",
    )(rows)


VMEM_SPEC = pl.BlockSpec(memory_space=pltpu.VMEM)
HBM_SPEC = pl.BlockSpec(memory_space=pltpu.HBM)


def columns(ref, i):
    width = ref.shape[1] // PIECES
    return ref.at[:, i * width : (i + 1) * width]


def lines(ref, i):
    height = ref.shape[0] // PIECES
    return ref.at[i * height : (i + 1) * height]


def two_parts(refs, i):
    first, second = refs
    width = 2 * first.shape[1] // PIECES
    ref = first if i < PIECES // 2 else second
    i = i % (PIECES // 2)
    return ref.at[:, i * width : (i + 1) * width]


def fetch(*moves):
    copies = []
    for i in range(PIECES):
        copies.append(
            [
                pltpu.make_async_copy(
                    two_parts(source, i) if isinstance(source, tuple) else cut(source, i),
                    cut(here, i),
                    sems.at[i],
                )
                for cut, source, here, sems in moves
            ]
        )
        for copy in copies[-1]:
            copy.start()
    return copies


def finish(copies):
    for copy in copies:
        copy.wait()


def store(copies, here_ref, target_ref, sem):
    copies.append(pltpu.make_async_copy(here_ref, target_ref, sem))
    copies[-1].start()


def encode_kernel(
    dev_slots,
    capacity,
    bias_ref,
    rows_f_ref,
    rows_g_ref,
    enc_ref,
    dec_ref,
    code_ref,
    slopes_ref,
    partial_ref,
    rows_here,
    enc_here,
    dec_here,
    code_here,
    slopes_here,
    out_here,
    sems,
):
    slots, latents = slopes_here.shape
    copies = fetch(
        (columns, (rows_f_ref, rows_g_ref), rows_here, sems.at[0]),
        (lines, enc_ref, enc_here, sems.at[1]),
    )
    dec_copies = fetch((columns, dec_ref, dec_here, sems.at[2]))
    preact = bias_ref[...]
    for i in range(PIECES):
        finish(copies[i])
        preact = preact + dot(columns(rows_here, i)[...], lines(enc_here, i)[...], 1, 0)
    output, slopes = activate(preact)
    row = lax.broadcasted_iota(jnp.int32, (slots, latents), 0)
    latent = lax.broadcasted_iota(jnp.int32, (slots, latents), 1)
    own = lax.div(lax.rem(row, dev_slots), capacity) == lax.div(latent, BLOCK)
    code = jnp.where(own, output, 0.0).astype(BF16)
    stores = []
    code_here[...] = code
    store(stores, code_here, code_ref, sems.at[3, 0])
    slopes_here[...] = jnp.where(own, slopes, 0.0)
    store(stores, slopes_here, slopes_ref, sems.at[3, 1])
    for i in range(PIECES):
        finish(dec_copies[i])
        columns(out_here, i)[...] = dot(code, columns(dec_here, i)[...], 1, 0).astype(BF16)
        store(stores, columns(out_here, i), columns(partial_ref, i), sems.at[4, i])
    finish(stores)


def encode(dev_slots, capacity, rows, enc_weight, enc_bias, dec_weight):
    slots = rows[0].shape[0]
    features, latents = enc_weight.shape
    return pl.pallas_call(
        lambda *refs: encode_kernel(dev_slots, capacity, *refs),
        out_shape=[
            pltpu.HBM((slots, latents), BF16),
            pltpu.HBM((slots, latents), F32),
            pltpu.HBM((slots, features), BF16),
        ],
        in_specs=[VMEM_SPEC] + [HBM_SPEC] * 4,
        out_specs=[HBM_SPEC] * 3,
        scratch_shapes=[
            pltpu.VMEM((slots, features), BF16),
            pltpu.VMEM((features, latents), BF16),
            pltpu.VMEM((latents, features), BF16),
            pltpu.VMEM((slots, latents), BF16),
            pltpu.VMEM((slots, latents), F32),
            pltpu.VMEM((slots, features), BF16),
            pltpu.SemaphoreType.DMA((5, PIECES)),
        ],
        cost_estimate=pl.CostEstimate(
            flops=4 * slots * latents * features,
            bytes_accessed=4 * features * (slots + latents),
            transcendentals=slots * latents,
        ),
        compiler_params=pltpu.CompilerParams(vmem_limit_bytes=62 * MIB),
        name="encode",
    )(enc_bias, *rows, enc_weight, dec_weight)


def home_kernel(
    select_ref,
    select_t_ref,
    bias_ref,
    act_ref,
    returned_ref,
    full_ref,
    errors_ref,
    send_ref,
    act_here,
    here_ref,
    full_out_ref,
    errors_out_ref,
    send_out_ref,
    sems,
):
    moves = fetch(
        (columns, returned_ref, here_ref, sems.at[0]), (columns, act_ref, act_here, sems.at[3])
    )
    stores = []
    for i, copies in enumerate(moves):
        finish(copies)
        full = dot(select_t_ref[...], columns(here_ref, i)[...], 1, 0) + columns(bias_ref, i)[...]
        errors = (full - columns(act_here, i)[...].astype(F32)).astype(BF16)
        if i < PIECES // 2:
            columns(errors_out_ref, i)[...] = errors
            out, target = columns(errors_out_ref, i), two_parts((errors_ref, send_ref), i)
        else:
            columns(send_out_ref, i)[...] = dot(select_ref[...], errors, 1, 0).astype(BF16)
            out, target = columns(send_out_ref, i), two_parts((errors_ref, send_ref), i)
        store(stores, out, target, sems.at[1, i])
        columns(full_out_ref, i)[...] = full.astype(BF16)
        store(stores, columns(full_out_ref, i), columns(full_ref, i), sems.at[2, i])
    finish(stores)


def rebuild(select, select_t, returned, activations, dec_bias):
    slots, tokens = select.shape
    features = activations.shape[1]
    return pl.pallas_call(
        home_kernel,
        out_shape=[
            pltpu.HBM((tokens, features), BF16),
            pltpu.HBM((tokens, features // 2), BF16),
            pltpu.HBM((slots, features // 2), BF16),
        ],
        in_specs=[VMEM_SPEC] * 3 + [HBM_SPEC] * 2,
        out_specs=[HBM_SPEC] * 3,
        scratch_shapes=[
            pltpu.VMEM((tokens, features), BF16),
            pltpu.VMEM((slots, features), BF16),
            pltpu.VMEM((tokens, features), BF16),
            pltpu.VMEM((tokens, features), BF16),
            pltpu.VMEM((slots, features), BF16),
            pltpu.SemaphoreType.DMA((4, PIECES)),
        ],
        cost_estimate=pl.CostEstimate(
            flops=4 * slots * tokens * features,
            bytes_accessed=4 * (slots + tokens) * features,
            transcendentals=0,
        ),
        compiler_params=pltpu.CompilerParams(vmem_limit_bytes=48 * MIB),
        name="rebuild",
    )(select, select_t, dec_bias, activations, returned)


def grads_kernel(
    count,
    squares_ref,
    code_t_ref,
    slopes_ref,
    dec_t_ref,
    rows_t_ref,
    got_f_ref,
    got_g_ref,
    dec_grad_ref,
    enc_grad_ref,
    bias_grad_ref,
    code_t_here,
    slopes_here,
    dec_t_here,
    rows_t_here,
    got_here,
    dec_out,
    enc_out,
    sems,
):
    first = []
    store(first, code_t_ref, code_t_here, sems.at[5, 0])
    copies = fetch(
        (columns, (got_f_ref, got_g_ref), got_here, sems.at[0]),
        (lines, dec_t_ref, dec_t_here, sems.at[1]),
    )
    second = []
    store(second, slopes_ref, slopes_here, sems.at[5, 1])
    scale = LOSS_SCALE / (squares_ref[0:1, 0:1] / count + 1e-06)
    finish(first)
    stores = []
    code_grad = None
    for i in range(PIECES):
        finish(copies[i])
        if i == 1:
            rows_copies = fetch((lines, rows_t_ref, rows_t_here, sems.at[2]))
        got = columns(got_here, i)[...]
        columns(dec_out, i)[...] = (dot(code_t_here[...], got, 1, 0) * scale).astype(BF16)
        store(stores, columns(dec_out, i), columns(dec_grad_ref, i), sems.at[3, i])
        part = dot(got, lines(dec_t_here, i)[...], 1, 0)
        code_grad = part if i == 0 else code_grad + part
    finish(second)
    code_grad = code_grad * (slopes_here[...] * scale)
    bias_grad_ref[...] = jnp.sum(code_grad, axis=0, keepdims=True)
    code_grad = code_grad.astype(BF16)
    for i in range(PIECES):
        finish(rows_copies[i])
        lines(enc_out, i)[...] = dot(lines(rows_t_here, i)[...], code_grad, 1, 0).astype(BF16)
        store(stores, lines(enc_out, i), lines(enc_grad_ref, i), sems.at[4, i])
    finish(stores)


def gradients(count, squares, code_t, slopes, dec_t, rows_t, got_errors):
    latents, slots = code_t.shape
    features = dec_t.shape[0]
    return pl.pallas_call(
        lambda *refs: grads_kernel(count, *refs),
        out_shape=[
            pltpu.HBM((latents, features), BF16),
            pltpu.HBM((features, latents), BF16),
            jax.ShapeDtypeStruct((1, latents), F32),
        ],
        in_specs=[VMEM_SPEC] + [HBM_SPEC] * 6,
        out_specs=[HBM_SPEC, HBM_SPEC, VMEM_SPEC],
        scratch_shapes=[
            pltpu.VMEM((latents, slots), BF16),
            pltpu.VMEM((slots, latents), F32),
            pltpu.VMEM((features, latents), BF16),
            pltpu.VMEM((features, slots), BF16),
            pltpu.VMEM((slots, features), BF16),
            pltpu.VMEM((latents, features), BF16),
            pltpu.VMEM((features, latents), BF16),
            pltpu.SemaphoreType.DMA((6, PIECES)),
        ],
        cost_estimate=pl.CostEstimate(
            flops=6 * slots * latents * features,
            bytes_accessed=2 * features * (2 * slots + 3 * latents),
            transcendentals=0,
        ),
        compiler_params=pltpu.CompilerParams(vmem_limit_bytes=60 * MIB),
        name="gradients",
    )(squares, code_t, slopes, dec_t, rows_t, *got_errors)


def per_device(activations, block_ids, enc_weight, enc_bias, dec_weight, dec_bias):
    tok_rows, feature_dim = activations.shape
    active_count = block_ids.shape[1]
    devices = lax.axis_size("lat")
    half = devices // 2
    local_latents = enc_weight.shape[1]
    blocks_dev = local_latents // BLOCK
    nblocks = blocks_dev * devices
    capacity = max(2, 3 * tok_rows * active_count // (2 * nblocks))
    dev_slots = blocks_dev * capacity
    half_slots = half * dev_slots
    side = feature_dim // 2

    def exchange(rows):
        return lax.all_to_all(rows, "lat", split_axis=0, concat_axis=0, tiled=True)

    def swap(rows, step=half):
        return lax.ppermute(rows, "lat", [(i, i ^ step) for i in range(devices)])

    def pick(select, rows):
        return dot(select, rows, 1, 0).astype(BF16)

    ids = block_ids.T
    order = jnp.arange(tok_rows, dtype=jnp.int32)
    same = jnp.any(ids[:, :, None, None] == ids.T[None, None, :, :], axis=3)
    same = same & (order[None, None, :] < order[None, :, None])
    slot_of = ids * capacity + jnp.sum(same.astype(jnp.int32), axis=2)
    slot_held = swap(slot_of)
    me = lax.axis_index("lat")
    slots = jnp.arange(2 * half_slots, dtype=jnp.int32)
    crossed = ((slots // dev_slots) ^ me) * dev_slots + slots % dev_slots

    def selection(slot, names):
        return jnp.any(names[:, None, None] == slot[None, :, :], axis=1).astype(BF16)

    select = selection(slot_of, slots)
    select_t = jnp.any(slots[None, None, :] == slot_of.T[:, :, None], axis=1).astype(BF16)
    select_own = selection(slot_of, crossed[:half_slots])
    select_held = selection(slot_held, crossed[:half_slots])
    by_swaps = half <= 8

    def deliver(tokens, by_slot_from, by_slot, value):
        if not by_swaps:
            return exchange(pick(select, tokens)), exchange(by_slot(by_slot_from)), value
        cuts = [slice(k * dev_slots, (k + 1) * dev_slots) for k in range(half)]
        own = [pick(select_own[cut], tokens) for cut in cuts]
        own = [own[0]] + list(together(*own[1:], by_slot_from))
        by_slot_from = own.pop()
        held = swap(tokens)
        got = exchange(by_slot(by_slot_from))
        held, value = together(held, value)
        rows = jnp.zeros((devices, dev_slots, tokens.shape[1]), BF16)
        far_first = list(range(half // 2, half)) + list(range(half // 2))
        for k in far_first:
            part = swap(own[k], k) if k else own[k]
            rows = lax.dynamic_update_index_in_dim(rows, part, me ^ k, 0)
        for k in far_first:
            part = pick(select_held[cuts[k]], held)
            part = swap(part, k) if k else part
            rows = lax.dynamic_update_index_in_dim(rows, part, me ^ (k + half), 0)
        return rows.reshape(devices * dev_slots, tokens.shape[1]), got, value

    act_f, act_g = activations[:, :side], activations[:, side:]
    rows_f, rows_g, squares = deliver(
        act_f, act_g, lambda rows: pick(select, rows), sum_of_squares(activations)
    )

    code_rows, slopes, partial_value = encode(
        dev_slots, capacity, (rows_f, rows_g), enc_weight, enc_bias[None, :], dec_weight
    )
    returned = exchange(partial_value)
    code_t = code_rows.T
    rows_t = jnp.concatenate([rows_f.T, rows_g.T], axis=0)

    dec_t = dec_weight.T
    steps = [1 << i for i in range((devices - 1).bit_length())]
    for step in steps[::-1]:
        squares = squares + swap(squares, step)
        if step == steps[-1]:
            squares, rows_t, code_t, dec_t = together(squares, rows_t, code_t, dec_t)
    returned, squares = together(returned, squares)
    full, err_f, send_g = rebuild(select, select_t, returned, activations, dec_bias[None, :])
    got_f, got_g, squares = deliver(err_f, send_g, lambda rows: rows, beside(squares))
    dec_grad, enc_grad, bias_grad = gradients(
        tok_rows * devices * feature_dim,
        squares,
        code_t,
        slopes,
        dec_t,
        rows_t,
        (got_f, got_g),
    )
    return (full, enc_grad, dec_grad, bias_grad.reshape(local_latents))


def solution(mesh):
    return jax.shard_map(
        per_device,
        mesh=mesh,
        in_specs=(
            P(("grp", "lat"), None),
            P(("grp", "lat"), None),
            P(None, "lat"),
            P("lat"),
            P("lat", None),
            P(),
        ),
        out_specs=(
            P(("grp", "lat"), None),
            P("grp", "lat"),
            P(("grp", "lat"), None),
            P(("grp", "lat")),
        ),
        check_vma=False,
    )
```

```python
import jax
import jax.numpy as jnp
from jax import lax
from jax.experimental import pallas as pl
from jax.experimental.pallas import tpu as pltpu
from jax.sharding import PartitionSpec as P

BLOCK = 64
LOSS_SCALE = 0.5
PIECES = 4
MIB = 1024 * 1024
F32 = jnp.float32
BF16 = jnp.bfloat16


def activate(preact):
    inner_arg = 0.7978845608 * (preact + 0.044715 * preact * preact * preact)
    tangent = jnp.tanh(inner_arg)
    output = 0.5 * preact * (1.0 + tangent)
    slopes = 0.5 * (1.0 + tangent) + 0.5 * preact * (1.0 - tangent * tangent) * 0.7978845608 * (
        1.0 + 0.134145 * preact * preact
    )
    return (output, slopes)


def dot(left, right, left_dim, right_dim):
    dims = (((left_dim,), (right_dim,)), ((), ()))
    return lax.dot_general(left, right, dims, preferred_element_type=F32)


def together(*values):
    return lax.optimization_barrier(values)


def squares_kernel(rows_ref, total_ref):
    total = jnp.zeros((8, 128), F32)
    rows, columns = rows_ref.shape
    for i in range(0, columns, 128):
        part = rows_ref[:, i : i + 128].astype(F32)
        total = total + jnp.sum((part * part).reshape(rows // 8, 8, 128), axis=0)
    total_ref[...] = jnp.full((8, 128), jnp.sum(total), F32)


def sum_of_squares(rows):
    return pl.pallas_call(
        squares_kernel,
        out_shape=jax.ShapeDtypeStruct((8, 128), F32),
        in_specs=[pl.BlockSpec(memory_space=pltpu.VMEM)],
        out_specs=pl.BlockSpec(memory_space=pltpu.VMEM),
        cost_estimate=pl.CostEstimate(
            flops=50_000_000_000, bytes_accessed=rows.size * 2, transcendentals=0
        ),
        name="squares",
    )(rows)


VMEM_SPEC = pl.BlockSpec(memory_space=pltpu.VMEM)
HBM_SPEC = pl.BlockSpec(memory_space=pltpu.HBM)


def columns(ref, i):
    width = ref.shape[1] // PIECES
    return ref.at[:, i * width : (i + 1) * width]


def lines(ref, i):
    height = ref.shape[0] // PIECES
    return ref.at[i * height : (i + 1) * height]


def two_parts(refs, i):
    first, second = refs
    width = 2 * first.shape[1] // PIECES
    ref = first if i < PIECES // 2 else second
    i = i % (PIECES // 2)
    return ref.at[:, i * width : (i + 1) * width]


def fetch(*moves):
    copies = []
    for i in range(PIECES):
        copies.append(
            [
                pltpu.make_async_copy(
                    two_parts(source, i) if isinstance(source, tuple) else cut(source, i),
                    cut(here, i),
                    sems.at[i],
                )
                for cut, source, here, sems in moves
            ]
        )
        for copy in copies[-1]:
            copy.start()
    return copies


def finish(copies):
    for copy in copies:
        copy.wait()


def store(copies, here_ref, target_ref, sem):
    copies.append(pltpu.make_async_copy(here_ref, target_ref, sem))
    copies[-1].start()


def encode_kernel(
    dev_slots,
    capacity,
    bias_ref,
    rows_f_ref,
    rows_g_ref,
    enc_ref,
    dec_ref,
    code_ref,
    slopes_ref,
    partial_ref,
    rows_here,
    enc_here,
    dec_here,
    code_here,
    slopes_here,
    out_here,
    sems,
):
    slots, latents = slopes_here.shape
    copies = fetch(
        (columns, (rows_f_ref, rows_g_ref), rows_here, sems.at[0]),
        (lines, enc_ref, enc_here, sems.at[1]),
    )
    dec_copies = fetch((columns, dec_ref, dec_here, sems.at[2]))
    preact = bias_ref[...]
    for i in range(PIECES):
        finish(copies[i])
        preact = preact + dot(columns(rows_here, i)[...], lines(enc_here, i)[...], 1, 0)
    output, slopes = activate(preact)
    row = lax.broadcasted_iota(jnp.int32, (slots, latents), 0)
    latent = lax.broadcasted_iota(jnp.int32, (slots, latents), 1)
    own = lax.div(lax.rem(row, dev_slots), capacity) == lax.div(latent, BLOCK)
    code = jnp.where(own, output, 0.0).astype(BF16)
    stores = []
    code_here[...] = code
    store(stores, code_here, code_ref, sems.at[3, 0])
    slopes_here[...] = jnp.where(own, slopes, 0.0)
    store(stores, slopes_here, slopes_ref, sems.at[3, 1])
    for i in range(PIECES):
        finish(dec_copies[i])
        columns(out_here, i)[...] = dot(code, columns(dec_here, i)[...], 1, 0).astype(BF16)
        store(stores, columns(out_here, i), columns(partial_ref, i), sems.at[4, i])
    finish(stores)


def encode(dev_slots, capacity, rows, enc_weight, enc_bias, dec_weight):
    slots = rows[0].shape[0]
    features, latents = enc_weight.shape
    return pl.pallas_call(
        lambda *refs: encode_kernel(dev_slots, capacity, *refs),
        out_shape=[
            pltpu.HBM((slots, latents), BF16),
            pltpu.HBM((slots, latents), F32),
            pltpu.HBM((slots, features), BF16),
        ],
        in_specs=[VMEM_SPEC] + [HBM_SPEC] * 4,
        out_specs=[HBM_SPEC] * 3,
        scratch_shapes=[
            pltpu.VMEM((slots, features), BF16),
            pltpu.VMEM((features, latents), BF16),
            pltpu.VMEM((latents, features), BF16),
            pltpu.VMEM((slots, latents), BF16),
            pltpu.VMEM((slots, latents), F32),
            pltpu.VMEM((slots, features), BF16),
            pltpu.SemaphoreType.DMA((5, PIECES)),
        ],
        cost_estimate=pl.CostEstimate(
            flops=4 * slots * latents * features,
            bytes_accessed=4 * features * (slots + latents),
            transcendentals=slots * latents,
        ),
        compiler_params=pltpu.CompilerParams(vmem_limit_bytes=62 * MIB),
        name="encode",
    )(enc_bias, *rows, enc_weight, dec_weight)


def home_kernel(
    select_ref,
    select_t_ref,
    bias_ref,
    act_ref,
    returned_ref,
    full_ref,
    send_ref,
    act_here,
    here_ref,
    full_out_ref,
    send_out_ref,
    sems,
):
    moves = fetch(
        (columns, returned_ref, here_ref, sems.at[0]), (columns, act_ref, act_here, sems.at[3])
    )
    stores = []
    for i, copies in enumerate(moves):
        finish(copies)
        full = dot(select_t_ref[...], columns(here_ref, i)[...], 1, 0) + columns(bias_ref, i)[...]
        errors = (full - columns(act_here, i)[...].astype(F32)).astype(BF16)
        columns(send_out_ref, i)[...] = dot(select_ref[...], errors, 1, 0).astype(BF16)
        store(stores, columns(send_out_ref, i), columns(send_ref, i), sems.at[1, i])
        columns(full_out_ref, i)[...] = full.astype(BF16)
        store(stores, columns(full_out_ref, i), columns(full_ref, i), sems.at[2, i])
    finish(stores)


def rebuild(select, select_t, returned, activations, dec_bias):
    slots, tokens = select.shape
    features = activations.shape[1]
    return pl.pallas_call(
        home_kernel,
        out_shape=[
            pltpu.HBM((tokens, features), BF16),
            pltpu.HBM((slots, features), BF16),
        ],
        in_specs=[VMEM_SPEC] * 3 + [HBM_SPEC] * 2,
        out_specs=[HBM_SPEC, HBM_SPEC],
        scratch_shapes=[
            pltpu.VMEM((tokens, features), BF16),
            pltpu.VMEM((slots, features), BF16),
            pltpu.VMEM((tokens, features), BF16),
            pltpu.VMEM((slots, features), BF16),
            pltpu.SemaphoreType.DMA((4, PIECES)),
        ],
        cost_estimate=pl.CostEstimate(
            flops=4 * slots * tokens * features,
            bytes_accessed=4 * (slots + tokens) * features,
            transcendentals=0,
        ),
        compiler_params=pltpu.CompilerParams(vmem_limit_bytes=48 * MIB),
        name="rebuild",
    )(select, select_t, dec_bias, activations, returned)


def grads_kernel(
    count,
    squares_ref,
    code_t_ref,
    slopes_ref,
    dec_t_ref,
    rows_t_ref,
    got_ref,
    dec_grad_ref,
    enc_grad_ref,
    bias_grad_ref,
    code_t_here,
    slopes_here,
    dec_t_here,
    rows_t_here,
    got_here,
    dec_out,
    enc_out,
    sems,
):
    first = []
    store(first, code_t_ref, code_t_here, sems.at[5, 0])
    copies = fetch(
        (columns, got_ref, got_here, sems.at[0]),
        (lines, dec_t_ref, dec_t_here, sems.at[1]),
    )
    second = []
    store(second, slopes_ref, slopes_here, sems.at[5, 1])
    scale = LOSS_SCALE / (squares_ref[0:1, 0:1] / count + 1e-06)
    finish(first)
    stores = []
    code_grad = None
    for i in range(PIECES):
        finish(copies[i])
        if i == 1:
            rows_copies = fetch((lines, rows_t_ref, rows_t_here, sems.at[2]))
        got = columns(got_here, i)[...]
        columns(dec_out, i)[...] = (dot(code_t_here[...], got, 1, 0) * scale).astype(BF16)
        store(stores, columns(dec_out, i), columns(dec_grad_ref, i), sems.at[3, i])
        part = dot(got, lines(dec_t_here, i)[...], 1, 0)
        code_grad = part if i == 0 else code_grad + part
    finish(second)
    code_grad = code_grad * (slopes_here[...] * scale)
    bias_grad_ref[...] = jnp.sum(code_grad, axis=0, keepdims=True)
    code_grad = code_grad.astype(BF16)
    for i in range(PIECES):
        finish(rows_copies[i])
        lines(enc_out, i)[...] = dot(lines(rows_t_here, i)[...], code_grad, 1, 0).astype(BF16)
        store(stores, lines(enc_out, i), lines(enc_grad_ref, i), sems.at[4, i])
    finish(stores)


def gradients(count, squares, code_t, slopes, dec_t, rows_t, got_errors):
    latents, slots = code_t.shape
    features = dec_t.shape[0]
    return pl.pallas_call(
        lambda *refs: grads_kernel(count, *refs),
        out_shape=[
            pltpu.HBM((latents, features), BF16),
            pltpu.HBM((features, latents), BF16),
            jax.ShapeDtypeStruct((1, latents), F32),
        ],
        in_specs=[VMEM_SPEC] + [HBM_SPEC] * 5,
        out_specs=[HBM_SPEC, HBM_SPEC, VMEM_SPEC],
        scratch_shapes=[
            pltpu.VMEM((latents, slots), BF16),
            pltpu.VMEM((slots, latents), F32),
            pltpu.VMEM((features, latents), BF16),
            pltpu.VMEM((features, slots), BF16),
            pltpu.VMEM((slots, features), BF16),
            pltpu.VMEM((latents, features), BF16),
            pltpu.VMEM((features, latents), BF16),
            pltpu.SemaphoreType.DMA((6, PIECES)),
        ],
        cost_estimate=pl.CostEstimate(
            flops=6 * slots * latents * features,
            bytes_accessed=2 * features * (2 * slots + 3 * latents),
            transcendentals=0,
        ),
        compiler_params=pltpu.CompilerParams(vmem_limit_bytes=60 * MIB),
        name="gradients",
    )(squares, code_t, slopes, dec_t, rows_t, got_errors)


def per_device(activations, block_ids, enc_weight, enc_bias, dec_weight, dec_bias):
    tok_rows, feature_dim = activations.shape
    active_count = block_ids.shape[1]
    devices = lax.axis_size("lat")
    half = devices // 2
    local_latents = enc_weight.shape[1]
    blocks_dev = local_latents // BLOCK
    nblocks = blocks_dev * devices
    capacity = max(2, 3 * tok_rows * active_count // (2 * nblocks))
    dev_slots = blocks_dev * capacity
    half_slots = half * dev_slots
    side = feature_dim // 2

    def exchange(rows):
        return lax.all_to_all(rows, "lat", split_axis=0, concat_axis=0, tiled=True)

    def swap(rows, step=half):
        return lax.ppermute(rows, "lat", [(i, i ^ step) for i in range(devices)])

    def pick(select, rows):
        return dot(select, rows, 1, 0).astype(BF16)

    ids = block_ids.T
    order = jnp.arange(tok_rows, dtype=jnp.int32)
    same = jnp.any(ids[:, :, None, None] == ids.T[None, None, :, :], axis=3)
    same = same & (order[None, None, :] < order[None, :, None])
    slot_of = ids * capacity + jnp.sum(same.astype(jnp.int32), axis=2)
    slot_held = swap(slot_of)
    me = lax.axis_index("lat")
    slots = jnp.arange(2 * half_slots, dtype=jnp.int32)
    crossed = ((slots // dev_slots) ^ me) * dev_slots + slots % dev_slots

    def selection(slot, names):
        return jnp.any(names[:, None, None] == slot[None, :, :], axis=1).astype(BF16)

    select = selection(slot_of, slots)
    select_t = jnp.any(slots[None, None, :] == slot_of.T[:, :, None], axis=1).astype(BF16)
    select_own = selection(slot_of, crossed[:half_slots])
    select_held = selection(slot_held, crossed[:half_slots])
    by_swaps = half <= 8

    def deliver(tokens, by_slot_from, by_slot, value):
        if not by_swaps:
            return exchange(pick(select, tokens)), exchange(by_slot(by_slot_from)), value
        cuts = [slice(k * dev_slots, (k + 1) * dev_slots) for k in range(half)]
        own = [pick(select_own[cut], tokens) for cut in cuts]
        own = [own[0]] + list(together(*own[1:], by_slot_from))
        by_slot_from = own.pop()
        held = swap(tokens)
        got = exchange(by_slot(by_slot_from))
        held, value = together(held, value)
        rows = jnp.zeros((devices, dev_slots, tokens.shape[1]), BF16)
        far_first = list(range(half // 2, half)) + list(range(half // 2))
        for k in far_first:
            part = swap(own[k], k) if k else own[k]
            rows = lax.dynamic_update_index_in_dim(rows, part, me ^ k, 0)
        for k in far_first:
            part = pick(select_held[cuts[k]], held)
            part = swap(part, k) if k else part
            rows = lax.dynamic_update_index_in_dim(rows, part, me ^ (k + half), 0)
        return rows.reshape(devices * dev_slots, tokens.shape[1]), got, value

    act_f, act_g = activations[:, :side], activations[:, side:]
    rows_f, rows_g, squares = deliver(
        act_f, act_g, lambda rows: pick(select, rows), sum_of_squares(activations)
    )

    code_rows, slopes, partial_value = encode(
        dev_slots, capacity, (rows_f, rows_g), enc_weight, enc_bias[None, :], dec_weight
    )
    returned = exchange(partial_value)
    step = 1
    while step < devices:
        squares = squares + swap(squares, step)
        step *= 2
    returned, squares = together(returned, squares)
    full, send_errors = rebuild(select, select_t, returned, activations, dec_bias[None, :])
    send_errors, code_rows, rows_f, rows_g, dec_rows = together(
        send_errors, code_rows, rows_f, rows_g, dec_weight
    )
    got_errors = exchange(send_errors)
    dec_grad, enc_grad, bias_grad = gradients(
        tok_rows * devices * feature_dim,
        squares,
        code_rows.T,
        slopes,
        dec_rows.T,
        jnp.concatenate([rows_f.T, rows_g.T], axis=0),
        got_errors,
    )
    return (full, enc_grad, dec_grad, bias_grad.reshape(local_latents))


def solution(mesh):
    return jax.shard_map(
        per_device,
        mesh=mesh,
        in_specs=(
            P(("grp", "lat"), None),
            P(("grp", "lat"), None),
            P(None, "lat"),
            P("lat"),
            P("lat", None),
            P(),
        ),
        out_specs=(
            P(("grp", "lat"), None),
            P("grp", "lat"),
            P(("grp", "lat"), None),
            P(("grp", "lat")),
        ),
        check_vma=False,
    )
```

```python
import jax
import jax.numpy as jnp
from jax import lax
from jax.experimental import pallas as pl
from jax.experimental.pallas import tpu as pltpu
from jax.sharding import PartitionSpec as P

BLOCK = 64
LOSS_SCALE = 0.5
PIECES = 4
MIB = 1024 * 1024
F32 = jnp.float32
BF16 = jnp.bfloat16


def activate(preact):
    inner_arg = 0.7978845608 * (preact + 0.044715 * preact * preact * preact)
    tangent = jnp.tanh(inner_arg)
    output = 0.5 * preact * (1.0 + tangent)
    slopes = 0.5 * (1.0 + tangent) + 0.5 * preact * (1.0 - tangent * tangent) * 0.7978845608 * (
        1.0 + 0.134145 * preact * preact
    )
    return (output, slopes)


def dot(left, right, left_dim, right_dim):
    dims = (((left_dim,), (right_dim,)), ((), ()))
    return lax.dot_general(left, right, dims, preferred_element_type=F32)


def together(*values):
    return lax.optimization_barrier(values)


def squares_kernel(rows_ref, total_ref):
    total = jnp.zeros((8, 128), F32)
    rows, columns = rows_ref.shape
    for i in range(0, columns, 128):
        part = rows_ref[:, i : i + 128].astype(F32)
        total = total + jnp.sum((part * part).reshape(rows // 8, 8, 128), axis=0)
    total_ref[...] = jnp.full((8, 128), jnp.sum(total), F32)


def sum_of_squares(rows):
    return pl.pallas_call(
        squares_kernel,
        out_shape=jax.ShapeDtypeStruct((8, 128), F32),
        in_specs=[pl.BlockSpec(memory_space=pltpu.VMEM)],
        out_specs=pl.BlockSpec(memory_space=pltpu.VMEM),
        cost_estimate=pl.CostEstimate(
            flops=50_000_000_000, bytes_accessed=rows.size * 2, transcendentals=0
        ),
        name="squares",
    )(rows)


VMEM_SPEC = pl.BlockSpec(memory_space=pltpu.VMEM)
HBM_SPEC = pl.BlockSpec(memory_space=pltpu.HBM)


def columns(ref, i):
    width = ref.shape[1] // PIECES
    return ref.at[:, i * width : (i + 1) * width]


def lines(ref, i):
    height = ref.shape[0] // PIECES
    return ref.at[i * height : (i + 1) * height]


def two_parts(refs, i):
    first, second = refs
    width = 2 * first.shape[1] // PIECES
    ref = first if i < PIECES // 2 else second
    i = i % (PIECES // 2)
    return ref.at[:, i * width : (i + 1) * width]


def fetch(*moves):
    copies = []
    for i in range(PIECES):
        copies.append(
            [
                pltpu.make_async_copy(
                    two_parts(source, i) if isinstance(source, tuple) else cut(source, i),
                    cut(here, i),
                    sems.at[i],
                )
                for cut, source, here, sems in moves
            ]
        )
        for copy in copies[-1]:
            copy.start()
    return copies


def finish(copies):
    for copy in copies:
        copy.wait()


def store(copies, here_ref, target_ref, sem):
    copies.append(pltpu.make_async_copy(here_ref, target_ref, sem))
    copies[-1].start()


def encode_kernel(
    dev_slots,
    capacity,
    bias_ref,
    rows_f_ref,
    rows_g_ref,
    enc_ref,
    dec_ref,
    code_ref,
    slopes_ref,
    partial_ref,
    rows_here,
    enc_here,
    dec_here,
    code_here,
    slopes_here,
    out_here,
    sems,
):
    slots, latents = slopes_here.shape
    copies = fetch(
        (columns, (rows_f_ref, rows_g_ref), rows_here, sems.at[0]),
        (lines, enc_ref, enc_here, sems.at[1]),
    )
    dec_copies = fetch((columns, dec_ref, dec_here, sems.at[2]))
    preact = bias_ref[...]
    for i in range(PIECES):
        finish(copies[i])
        preact = preact + dot(columns(rows_here, i)[...], lines(enc_here, i)[...], 1, 0)
    output, slopes = activate(preact)
    row = lax.broadcasted_iota(jnp.int32, (slots, latents), 0)
    latent = lax.broadcasted_iota(jnp.int32, (slots, latents), 1)
    own = lax.div(lax.rem(row, dev_slots), capacity) == lax.div(latent, BLOCK)
    code = jnp.where(own, output, 0.0).astype(BF16)
    stores = []
    code_here[...] = code
    store(stores, code_here, code_ref, sems.at[3, 0])
    slopes_here[...] = jnp.where(own, slopes, 0.0)
    store(stores, slopes_here, slopes_ref, sems.at[3, 1])
    for i in range(PIECES):
        finish(dec_copies[i])
        columns(out_here, i)[...] = dot(code, columns(dec_here, i)[...], 1, 0).astype(BF16)
        store(stores, columns(out_here, i), columns(partial_ref, i), sems.at[4, i])
    finish(stores)


def encode(dev_slots, capacity, rows, enc_weight, enc_bias, dec_weight):
    slots = rows[0].shape[0]
    features, latents = enc_weight.shape
    return pl.pallas_call(
        lambda *refs: encode_kernel(dev_slots, capacity, *refs),
        out_shape=[
            pltpu.HBM((slots, latents), BF16),
            pltpu.HBM((slots, latents), F32),
            pltpu.HBM((slots, features), BF16),
        ],
        in_specs=[VMEM_SPEC] + [HBM_SPEC] * 4,
        out_specs=[HBM_SPEC] * 3,
        scratch_shapes=[
            pltpu.VMEM((slots, features), BF16),
            pltpu.VMEM((features, latents), BF16),
            pltpu.VMEM((latents, features), BF16),
            pltpu.VMEM((slots, latents), BF16),
            pltpu.VMEM((slots, latents), F32),
            pltpu.VMEM((slots, features), BF16),
            pltpu.SemaphoreType.DMA((5, PIECES)),
        ],
        cost_estimate=pl.CostEstimate(
            flops=4 * slots * latents * features,
            bytes_accessed=4 * features * (slots + latents),
            transcendentals=slots * latents,
        ),
        compiler_params=pltpu.CompilerParams(vmem_limit_bytes=62 * MIB),
        name="encode",
    )(enc_bias, *rows, enc_weight, dec_weight)


def home_kernel(
    select_ref,
    select_t_ref,
    bias_ref,
    act_ref,
    returned_ref,
    full_ref,
    send_ref,
    act_here,
    here_ref,
    full_out_ref,
    send_out_ref,
    sems,
):
    moves = fetch(
        (columns, returned_ref, here_ref, sems.at[0]), (columns, act_ref, act_here, sems.at[3])
    )
    stores = []
    for i, copies in enumerate(moves):
        finish(copies)
        full = dot(select_t_ref[...], columns(here_ref, i)[...], 1, 0) + columns(bias_ref, i)[...]
        errors = (full - columns(act_here, i)[...].astype(F32)).astype(BF16)
        columns(send_out_ref, i)[...] = dot(select_ref[...], errors, 1, 0).astype(BF16)
        store(stores, columns(send_out_ref, i), columns(send_ref, i), sems.at[1, i])
        columns(full_out_ref, i)[...] = full.astype(BF16)
        store(stores, columns(full_out_ref, i), columns(full_ref, i), sems.at[2, i])
    finish(stores)


def rebuild(select, select_t, returned, activations, dec_bias):
    slots, tokens = select.shape
    features = activations.shape[1]
    return pl.pallas_call(
        home_kernel,
        out_shape=[
            pltpu.HBM((tokens, features), BF16),
            pltpu.HBM((slots, features), BF16),
        ],
        in_specs=[VMEM_SPEC] * 3 + [HBM_SPEC] * 2,
        out_specs=[HBM_SPEC, HBM_SPEC],
        scratch_shapes=[
            pltpu.VMEM((tokens, features), BF16),
            pltpu.VMEM((slots, features), BF16),
            pltpu.VMEM((tokens, features), BF16),
            pltpu.VMEM((slots, features), BF16),
            pltpu.SemaphoreType.DMA((4, PIECES)),
        ],
        cost_estimate=pl.CostEstimate(
            flops=4 * slots * tokens * features,
            bytes_accessed=4 * (slots + tokens) * features,
            transcendentals=0,
        ),
        compiler_params=pltpu.CompilerParams(vmem_limit_bytes=48 * MIB),
        name="rebuild",
    )(select, select_t, dec_bias, activations, returned)


def grads_kernel(
    count,
    squares_ref,
    code_t_ref,
    slopes_ref,
    dec_t_ref,
    rows_t_ref,
    got_ref,
    dec_grad_ref,
    enc_grad_ref,
    bias_grad_ref,
    code_t_here,
    slopes_here,
    dec_t_here,
    rows_t_here,
    got_here,
    dec_out,
    enc_out,
    sems,
):
    first = []
    store(first, code_t_ref, code_t_here, sems.at[5, 0])
    copies = fetch(
        (columns, got_ref, got_here, sems.at[0]),
        (lines, dec_t_ref, dec_t_here, sems.at[1]),
    )
    second = []
    store(second, slopes_ref, slopes_here, sems.at[5, 1])
    scale = LOSS_SCALE / (squares_ref[0:1, 0:1] / count + 1e-06)
    finish(first)
    stores = []
    code_grad = None
    for i in range(PIECES):
        finish(copies[i])
        if i == 1:
            rows_copies = fetch((lines, rows_t_ref, rows_t_here, sems.at[2]))
        got = columns(got_here, i)[...]
        columns(dec_out, i)[...] = (dot(code_t_here[...], got, 1, 0) * scale).astype(BF16)
        store(stores, columns(dec_out, i), columns(dec_grad_ref, i), sems.at[3, i])
        part = dot(got, lines(dec_t_here, i)[...], 1, 0)
        code_grad = part if i == 0 else code_grad + part
    finish(second)
    code_grad = code_grad * (slopes_here[...] * scale)
    bias_grad_ref[...] = jnp.sum(code_grad, axis=0, keepdims=True)
    code_grad = code_grad.astype(BF16)
    for i in range(PIECES):
        finish(rows_copies[i])
        lines(enc_out, i)[...] = dot(lines(rows_t_here, i)[...], code_grad, 1, 0).astype(BF16)
        store(stores, lines(enc_out, i), lines(enc_grad_ref, i), sems.at[4, i])
    finish(stores)


def gradients(count, squares, code_t, slopes, dec_t, rows_t, got_errors):
    latents, slots = code_t.shape
    features = dec_t.shape[0]
    return pl.pallas_call(
        lambda *refs: grads_kernel(count, *refs),
        out_shape=[
            pltpu.HBM((latents, features), BF16),
            pltpu.HBM((features, latents), BF16),
            jax.ShapeDtypeStruct((1, latents), F32),
        ],
        in_specs=[VMEM_SPEC] + [HBM_SPEC] * 5,
        out_specs=[HBM_SPEC, HBM_SPEC, VMEM_SPEC],
        scratch_shapes=[
            pltpu.VMEM((latents, slots), BF16),
            pltpu.VMEM((slots, latents), F32),
            pltpu.VMEM((features, latents), BF16),
            pltpu.VMEM((features, slots), BF16),
            pltpu.VMEM((slots, features), BF16),
            pltpu.VMEM((latents, features), BF16),
            pltpu.VMEM((features, latents), BF16),
            pltpu.SemaphoreType.DMA((6, PIECES)),
        ],
        cost_estimate=pl.CostEstimate(
            flops=6 * slots * latents * features,
            bytes_accessed=2 * features * (2 * slots + 3 * latents),
            transcendentals=0,
        ),
        compiler_params=pltpu.CompilerParams(vmem_limit_bytes=62 * MIB),
        name="gradients",
    )(squares, code_t, slopes, dec_t, rows_t, got_errors)


def per_device(activations, block_ids, enc_weight, enc_bias, dec_weight, dec_bias):
    tok_rows, feature_dim = activations.shape
    active_count = block_ids.shape[1]
    devices = lax.axis_size("lat")
    half = devices // 2
    local_latents = enc_weight.shape[1]
    blocks_dev = local_latents // BLOCK
    nblocks = blocks_dev * devices
    capacity = max(2, 3 * tok_rows * active_count // (2 * nblocks))
    dev_slots = blocks_dev * capacity
    half_slots = half * dev_slots
    side = feature_dim // 2

    def exchange(rows):
        return lax.all_to_all(rows, "lat", split_axis=0, concat_axis=0, tiled=True)

    def swap(rows, step=half):
        return lax.ppermute(rows, "lat", [(i, i ^ step) for i in range(devices)])

    def pick(select, rows):
        return dot(select, rows, 1, 0).astype(BF16)

    ids = block_ids.T
    order = jnp.arange(tok_rows, dtype=jnp.int32)
    same = jnp.any(ids[:, :, None, None] == ids.T[None, None, :, :], axis=3)
    same = same & (order[None, None, :] < order[None, :, None])
    slot_of = ids * capacity + jnp.sum(same.astype(jnp.int32), axis=2)
    slot_held = swap(slot_of)
    me = lax.axis_index("lat")
    slots = jnp.arange(2 * half_slots, dtype=jnp.int32)
    crossed = ((slots // dev_slots) ^ me) * dev_slots + slots % dev_slots

    def selection(slot, names):
        return jnp.any(names[:, None, None] == slot[None, :, :], axis=1).astype(BF16)

    select = selection(slot_of, slots)
    select_t = jnp.any(slots[None, None, :] == slot_of.T[:, :, None], axis=1).astype(BF16)
    select_own = selection(slot_of, crossed[:half_slots])
    select_held = selection(slot_held, crossed[:half_slots])
    by_swaps = half <= 8

    def deliver(tokens, by_slot_from, by_slot, value):
        if not by_swaps:
            return exchange(pick(select, tokens)), exchange(by_slot(by_slot_from)), value
        cuts = [slice(k * dev_slots, (k + 1) * dev_slots) for k in range(half)]
        own = [pick(select_own[cut], tokens) for cut in cuts]
        own = [own[0]] + list(together(*own[1:], by_slot_from))
        by_slot_from = own.pop()
        held = swap(tokens)
        got = exchange(by_slot(by_slot_from))
        far = list(range(half // 2, half))
        near = list(range(half // 2))
        own = own[: half // 2] + [swap(own[k], k) for k in far]
        held, value, *own[half // 2 :] = together(held, value, *own[half // 2 :])
        rows = jnp.zeros((devices, dev_slots, tokens.shape[1]), BF16)
        for k in far:
            rows = lax.dynamic_update_index_in_dim(rows, own[k], me ^ k, 0)
        for k in far + near:
            part = pick(select_held[cuts[k]], held)
            part = swap(part, k) if k else part
            rows = lax.dynamic_update_index_in_dim(rows, part, me ^ (k + half), 0)
        for k in near:
            part = swap(own[k], k) if k else own[k]
            rows = lax.dynamic_update_index_in_dim(rows, part, me ^ k, 0)
        return rows.reshape(devices * dev_slots, tokens.shape[1]), got, value

    act_f, act_g = activations[:, :side], activations[:, side:]
    rows_f, rows_g, squares = deliver(
        act_f, act_g, lambda rows: pick(select, rows), sum_of_squares(activations)
    )

    code_rows, slopes, partial_value = encode(
        dev_slots, capacity, (rows_f, rows_g), enc_weight, enc_bias[None, :], dec_weight
    )
    returned = exchange(partial_value)
    step = 1
    while step < devices:
        squares = squares + swap(squares, step)
        step *= 2
    returned, squares = together(returned, squares)
    full, send_errors = rebuild(select, select_t, returned, activations, dec_bias[None, :])
    send_errors, code_rows, rows_f, rows_g, dec_rows = together(
        send_errors, code_rows, rows_f, rows_g, dec_weight
    )
    got_errors = exchange(send_errors)
    dec_grad, enc_grad, bias_grad = gradients(
        tok_rows * devices * feature_dim,
        squares,
        code_rows.T,
        slopes,
        dec_rows.T,
        jnp.concatenate([rows_f.T, rows_g.T], axis=0),
        got_errors,
    )
    return (full, enc_grad, dec_grad, bias_grad.reshape(local_latents))


def solution(mesh):
    return jax.shard_map(
        per_device,
        mesh=mesh,
        in_specs=(
            P(("grp", "lat"), None),
            P(("grp", "lat"), None),
            P(None, "lat"),
            P("lat"),
            P("lat", None),
            P(),
        ),
        out_specs=(
            P(("grp", "lat"), None),
            P("grp", "lat"),
            P(("grp", "lat"), None),
            P(("grp", "lat")),
        ),
        check_vma=False,
    )
```

```python
import jax
import jax.numpy as jnp
from jax import lax
from jax.experimental import pallas as pl
from jax.experimental.pallas import tpu as pltpu
from jax.sharding import PartitionSpec as P

BLOCK = 64
LOSS_SCALE = 0.5
PIECES = 4
MIB = 1024 * 1024
F32 = jnp.float32
BF16 = jnp.bfloat16


def activate(preact):
    inner_arg = 0.7978845608 * (preact + 0.044715 * preact * preact * preact)
    tangent = jnp.tanh(inner_arg)
    output = 0.5 * preact * (1.0 + tangent)
    slopes = 0.5 * (1.0 + tangent) + 0.5 * preact * (1.0 - tangent * tangent) * 0.7978845608 * (
        1.0 + 0.134145 * preact * preact
    )
    return (output, slopes)


def dot(left, right, left_dim, right_dim):
    dims = (((left_dim,), (right_dim,)), ((), ()))
    return lax.dot_general(left, right, dims, preferred_element_type=F32)


def together(*values):
    return lax.optimization_barrier(values)


def squares_kernel(rows_ref, total_ref):
    total = jnp.zeros((8, 128), F32)
    rows, columns = rows_ref.shape
    for i in range(0, columns, 128):
        part = rows_ref[:, i : i + 128].astype(F32)
        total = total + jnp.sum((part * part).reshape(rows // 8, 8, 128), axis=0)
    total_ref[...] = jnp.full((8, 128), jnp.sum(total), F32)


def sum_of_squares(rows):
    return pl.pallas_call(
        squares_kernel,
        out_shape=jax.ShapeDtypeStruct((8, 128), F32),
        in_specs=[pl.BlockSpec(memory_space=pltpu.VMEM)],
        out_specs=pl.BlockSpec(memory_space=pltpu.VMEM),
        cost_estimate=pl.CostEstimate(
            flops=50_000_000_000, bytes_accessed=rows.size * 2, transcendentals=0
        ),
        name="squares",
    )(rows)


VMEM_SPEC = pl.BlockSpec(memory_space=pltpu.VMEM)
HBM_SPEC = pl.BlockSpec(memory_space=pltpu.HBM)


def columns(ref, i):
    width = ref.shape[1] // PIECES
    return ref.at[:, i * width : (i + 1) * width]


def lines(ref, i):
    height = ref.shape[0] // PIECES
    return ref.at[i * height : (i + 1) * height]


def two_parts(refs, i):
    first, second = refs
    width = 2 * first.shape[1] // PIECES
    ref = first if i < PIECES // 2 else second
    i = i % (PIECES // 2)
    return ref.at[:, i * width : (i + 1) * width]


def fetch(*moves):
    copies = []
    for i in range(PIECES):
        copies.append(
            [
                pltpu.make_async_copy(
                    two_parts(source, i) if isinstance(source, tuple) else cut(source, i),
                    cut(here, i),
                    sems.at[i],
                )
                for cut, source, here, sems in moves
            ]
        )
        for copy in copies[-1]:
            copy.start()
    return copies


def finish(copies):
    for copy in copies:
        copy.wait()


def store(copies, here_ref, target_ref, sem):
    copies.append(pltpu.make_async_copy(here_ref, target_ref, sem))
    copies[-1].start()


def encode_kernel(
    dev_slots,
    capacity,
    bias_ref,
    rows_f_ref,
    rows_g_ref,
    enc_ref,
    dec_ref,
    code_ref,
    slopes_ref,
    partial_ref,
    rows_here,
    enc_here,
    dec_here,
    code_here,
    slopes_here,
    out_here,
    sems,
):
    slots, latents = slopes_here.shape
    copies = fetch(
        (columns, (rows_f_ref, rows_g_ref), rows_here, sems.at[0]),
        (lines, enc_ref, enc_here, sems.at[1]),
    )
    dec_copies = fetch((columns, dec_ref, dec_here, sems.at[2]))
    preact = bias_ref[...]
    for i in range(PIECES):
        finish(copies[i])
        preact = preact + dot(columns(rows_here, i)[...], lines(enc_here, i)[...], 1, 0)
    output, slopes = activate(preact)
    row = lax.broadcasted_iota(jnp.int32, (slots, latents), 0)
    latent = lax.broadcasted_iota(jnp.int32, (slots, latents), 1)
    own = lax.div(lax.rem(row, dev_slots), capacity) == lax.div(latent, BLOCK)
    code = jnp.where(own, output, 0.0).astype(BF16)
    stores = []
    code_here[...] = code
    store(stores, code_here, code_ref, sems.at[3, 0])
    slopes_here[...] = jnp.where(own, slopes, 0.0)
    store(stores, slopes_here, slopes_ref, sems.at[3, 1])
    for i in range(PIECES):
        finish(dec_copies[i])
        columns(out_here, i)[...] = dot(code, columns(dec_here, i)[...], 1, 0).astype(BF16)
        store(stores, columns(out_here, i), columns(partial_ref, i), sems.at[4, i])
    finish(stores)


def encode(dev_slots, capacity, rows, enc_weight, enc_bias, dec_weight):
    slots = rows[0].shape[0]
    features, latents = enc_weight.shape
    return pl.pallas_call(
        lambda *refs: encode_kernel(dev_slots, capacity, *refs),
        out_shape=[
            pltpu.HBM((slots, latents), BF16),
            pltpu.HBM((slots, latents), F32),
            pltpu.HBM((slots, features), BF16),
        ],
        in_specs=[VMEM_SPEC] + [HBM_SPEC] * 4,
        out_specs=[HBM_SPEC] * 3,
        scratch_shapes=[
            pltpu.VMEM((slots, features), BF16),
            pltpu.VMEM((features, latents), BF16),
            pltpu.VMEM((latents, features), BF16),
            pltpu.VMEM((slots, latents), BF16),
            pltpu.VMEM((slots, latents), F32),
            pltpu.VMEM((slots, features), BF16),
            pltpu.SemaphoreType.DMA((5, PIECES)),
        ],
        cost_estimate=pl.CostEstimate(
            flops=4 * slots * latents * features,
            bytes_accessed=4 * features * (slots + latents),
            transcendentals=slots * latents,
        ),
        compiler_params=pltpu.CompilerParams(vmem_limit_bytes=62 * MIB),
        name="encode",
    )(enc_bias, *rows, enc_weight, dec_weight)


def home_kernel(
    select_ref,
    select_t_ref,
    bias_ref,
    act_ref,
    returned_ref,
    full_ref,
    send_ref,
    act_here,
    here_ref,
    full_out_ref,
    send_out_ref,
    sems,
):
    moves = fetch(
        (columns, returned_ref, here_ref, sems.at[0]), (columns, act_ref, act_here, sems.at[3])
    )
    stores = []
    for i, copies in enumerate(moves):
        finish(copies)
        full = dot(select_t_ref[...], columns(here_ref, i)[...], 1, 0) + columns(bias_ref, i)[...]
        errors = (full - columns(act_here, i)[...].astype(F32)).astype(BF16)
        columns(send_out_ref, i)[...] = dot(select_ref[...], errors, 1, 0).astype(BF16)
        store(stores, columns(send_out_ref, i), columns(send_ref, i), sems.at[1, i])
        columns(full_out_ref, i)[...] = full.astype(BF16)
        store(stores, columns(full_out_ref, i), columns(full_ref, i), sems.at[2, i])
    finish(stores)


def rebuild(select, select_t, returned, activations, dec_bias):
    slots, tokens = select.shape
    features = activations.shape[1]
    return pl.pallas_call(
        home_kernel,
        out_shape=[
            pltpu.HBM((tokens, features), BF16),
            pltpu.HBM((slots, features), BF16),
        ],
        in_specs=[VMEM_SPEC] * 3 + [HBM_SPEC] * 2,
        out_specs=[HBM_SPEC, HBM_SPEC],
        scratch_shapes=[
            pltpu.VMEM((tokens, features), BF16),
            pltpu.VMEM((slots, features), BF16),
            pltpu.VMEM((tokens, features), BF16),
            pltpu.VMEM((slots, features), BF16),
            pltpu.SemaphoreType.DMA((4, PIECES)),
        ],
        cost_estimate=pl.CostEstimate(
            flops=4 * slots * tokens * features,
            bytes_accessed=4 * (slots + tokens) * features,
            transcendentals=0,
        ),
        compiler_params=pltpu.CompilerParams(vmem_limit_bytes=48 * MIB),
        name="rebuild",
    )(select, select_t, dec_bias, activations, returned)


def grads_kernel(
    count,
    squares_ref,
    code_t_ref,
    slopes_ref,
    dec_t_ref,
    rows_t_ref,
    got_ref,
    dec_grad_ref,
    enc_grad_ref,
    bias_grad_ref,
    code_t_here,
    slopes_here,
    dec_t_here,
    rows_t_here,
    got_here,
    dec_out,
    enc_out,
    sems,
):
    first = []
    store(first, code_t_ref, code_t_here, sems.at[5, 0])
    copies = fetch(
        (columns, got_ref, got_here, sems.at[0]),
        (lines, dec_t_ref, dec_t_here, sems.at[1]),
    )
    second = []
    store(second, slopes_ref, slopes_here, sems.at[5, 1])
    scale = LOSS_SCALE / (squares_ref[0:1, 0:1] / count + 1e-06)
    finish(first)
    stores = []
    code_grad = None
    for i in range(PIECES):
        finish(copies[i])
        if i == 1:
            rows_copies = fetch((lines, rows_t_ref, rows_t_here, sems.at[2]))
        got = columns(got_here, i)[...]
        columns(dec_out, i)[...] = (dot(code_t_here[...], got, 1, 0) * scale).astype(BF16)
        store(stores, columns(dec_out, i), columns(dec_grad_ref, i), sems.at[3, i])
        part = dot(got, lines(dec_t_here, i)[...], 1, 0)
        code_grad = part if i == 0 else code_grad + part
    finish(second)
    code_grad = code_grad * (slopes_here[...] * scale)
    bias_grad_ref[...] = jnp.sum(code_grad, axis=0, keepdims=True)
    code_grad = code_grad.astype(BF16)
    for i in range(PIECES):
        finish(rows_copies[i])
        lines(enc_out, i)[...] = dot(lines(rows_t_here, i)[...], code_grad, 1, 0).astype(BF16)
        store(stores, lines(enc_out, i), lines(enc_grad_ref, i), sems.at[4, i])
    finish(stores)


def gradients(count, squares, code_t, slopes, dec_t, rows_t, got_errors):
    latents, slots = code_t.shape
    features = dec_t.shape[0]
    return pl.pallas_call(
        lambda *refs: grads_kernel(count, *refs),
        out_shape=[
            pltpu.HBM((latents, features), BF16),
            pltpu.HBM((features, latents), BF16),
            jax.ShapeDtypeStruct((1, latents), F32),
        ],
        in_specs=[VMEM_SPEC] + [HBM_SPEC] * 5,
        out_specs=[HBM_SPEC, HBM_SPEC, VMEM_SPEC],
        scratch_shapes=[
            pltpu.VMEM((latents, slots), BF16),
            pltpu.VMEM((slots, latents), F32),
            pltpu.VMEM((features, latents), BF16),
            pltpu.VMEM((features, slots), BF16),
            pltpu.VMEM((slots, features), BF16),
            pltpu.VMEM((latents, features), BF16),
            pltpu.VMEM((features, latents), BF16),
            pltpu.SemaphoreType.DMA((6, PIECES)),
        ],
        cost_estimate=pl.CostEstimate(
            flops=6 * slots * latents * features,
            bytes_accessed=2 * features * (2 * slots + 3 * latents),
            transcendentals=0,
        ),
        compiler_params=pltpu.CompilerParams(vmem_limit_bytes=62 * MIB),
        name="gradients",
    )(squares, code_t, slopes, dec_t, rows_t, got_errors)


def per_device(activations, block_ids, enc_weight, enc_bias, dec_weight, dec_bias):
    tok_rows, feature_dim = activations.shape
    active_count = block_ids.shape[1]
    devices = lax.axis_size("lat")
    half = devices // 2
    local_latents = enc_weight.shape[1]
    blocks_dev = local_latents // BLOCK
    nblocks = blocks_dev * devices
    capacity = max(2, 3 * tok_rows * active_count // (2 * nblocks))
    dev_slots = blocks_dev * capacity
    half_slots = half * dev_slots
    side = feature_dim // 2

    def exchange(rows):
        return lax.all_to_all(rows, "lat", split_axis=0, concat_axis=0, tiled=True)

    def swap(rows, step=half):
        return lax.ppermute(rows, "lat", [(i, i ^ step) for i in range(devices)])

    def pick(select, rows):
        return dot(select, rows, 1, 0).astype(BF16)

    ids = block_ids.T
    order = jnp.arange(tok_rows, dtype=jnp.int32)
    same = jnp.any(ids[:, :, None, None] == ids.T[None, None, :, :], axis=3)
    same = same & (order[None, None, :] < order[None, :, None])
    slot_of = ids * capacity + jnp.sum(same.astype(jnp.int32), axis=2)
    slot_held = swap(slot_of)
    me = lax.axis_index("lat")
    slots = jnp.arange(2 * half_slots, dtype=jnp.int32)
    crossed = ((slots // dev_slots) ^ me) * dev_slots + slots % dev_slots

    def selection(slot, names):
        return jnp.any(names[:, None, None] == slot[None, :, :], axis=1).astype(BF16)

    select = selection(slot_of, slots)
    select_t = jnp.any(slots[None, None, :] == slot_of.T[:, :, None], axis=1).astype(BF16)
    select_own = selection(slot_of, crossed[:half_slots])
    select_held = selection(slot_held, crossed[:half_slots])
    by_swaps = half <= 8

    def deliver(tokens, by_slot_from, by_slot, value):
        if not by_swaps:
            return exchange(pick(select, tokens)), exchange(by_slot(by_slot_from)), value
        cuts = [slice(k * dev_slots, (k + 1) * dev_slots) for k in range(half)]
        own = [pick(select_own[cut], tokens) for cut in cuts]
        own = [own[0]] + list(together(*own[1:], by_slot_from))
        by_slot_from = own.pop()
        held = swap(tokens)
        got = exchange(by_slot(by_slot_from))
        held, value = together(held, value)
        rows = jnp.zeros((devices, dev_slots, tokens.shape[1]), BF16)
        far_first = list(range(half // 2, half)) + list(range(half // 2))
        for k in far_first:
            part = swap(own[k], k) if k else own[k]
            rows = lax.dynamic_update_index_in_dim(rows, part, me ^ k, 0)
        for k in far_first:
            part = pick(select_held[cuts[k]], held)
            part = swap(part, k) if k else part
            rows = lax.dynamic_update_index_in_dim(rows, part, me ^ (k + half), 0)
        return rows.reshape(devices * dev_slots, tokens.shape[1]), got, value

    act_f, act_g = activations[:, :side], activations[:, side:]
    rows_f, rows_g, squares = deliver(
        act_f, act_g, lambda rows: pick(select, rows), sum_of_squares(activations)
    )

    code_rows, slopes, partial_value = encode(
        dev_slots, capacity, (rows_f, rows_g), enc_weight, enc_bias[None, :], dec_weight
    )
    returned = exchange(partial_value)
    step = 1
    while step < devices:
        squares = squares + swap(squares, step)
        step *= 2
    returned, squares = together(returned, squares)
    full, send_errors = rebuild(select, select_t, returned, activations, dec_bias[None, :])
    send_errors, code_rows, rows_f, rows_g, dec_rows = together(
        send_errors, code_rows, rows_f, rows_g, dec_weight
    )
    got_errors = exchange(send_errors)
    dec_grad, enc_grad, bias_grad = gradients(
        tok_rows * devices * feature_dim,
        squares,
        code_rows.T,
        slopes,
        dec_rows.T,
        jnp.concatenate([rows_f.T, rows_g.T], axis=0),
        got_errors,
    )
    return (full, enc_grad, dec_grad, bias_grad.reshape(local_latents))


def solution(mesh):
    return jax.shard_map(
        per_device,
        mesh=mesh,
        in_specs=(
            P(("grp", "lat"), None),
            P(("grp", "lat"), None),
            P(None, "lat"),
            P("lat"),
            P("lat", None),
            P(),
        ),
        out_specs=(
            P(("grp", "lat"), None),
            P("grp", "lat"),
            P(("grp", "lat"), None),
            P(("grp", "lat")),
        ),
        check_vma=False,
    )
```

```python
import jax
import jax.numpy as jnp
from jax import lax
from jax.experimental import pallas as pl
from jax.experimental.pallas import tpu as pltpu
from jax.sharding import PartitionSpec as P

BLOCK = 64
LOSS_SCALE = 0.5
PIECES = 4
MIB = 1024 * 1024
F32 = jnp.float32
BF16 = jnp.bfloat16


def activate(preact):
    inner_arg = 0.7978845608 * (preact + 0.044715 * preact * preact * preact)
    tangent = jnp.tanh(inner_arg)
    output = 0.5 * preact * (1.0 + tangent)
    slopes = 0.5 * (1.0 + tangent) + 0.5 * preact * (1.0 - tangent * tangent) * 0.7978845608 * (
        1.0 + 0.134145 * preact * preact
    )
    return (output, slopes)


def dot(left, right, left_dim, right_dim):
    dims = (((left_dim,), (right_dim,)), ((), ()))
    return lax.dot_general(left, right, dims, preferred_element_type=F32)


def together(*values):
    return lax.optimization_barrier(values)


def squares_kernel(rows_ref, total_ref):
    total = jnp.zeros((8, 128), F32)
    rows, columns = rows_ref.shape
    for i in range(0, columns, 128):
        part = rows_ref[:, i : i + 128].astype(F32)
        total = total + jnp.sum((part * part).reshape(rows // 8, 8, 128), axis=0)
    total_ref[...] = jnp.full((8, 128), jnp.sum(total), F32)


def sum_of_squares(rows):
    return pl.pallas_call(
        squares_kernel,
        out_shape=jax.ShapeDtypeStruct((8, 128), F32),
        in_specs=[pl.BlockSpec(memory_space=pltpu.VMEM)],
        out_specs=pl.BlockSpec(memory_space=pltpu.VMEM),
        cost_estimate=pl.CostEstimate(
            flops=50_000_000_000, bytes_accessed=rows.size * 2, transcendentals=0
        ),
        name="squares",
    )(rows)


VMEM_SPEC = pl.BlockSpec(memory_space=pltpu.VMEM)
HBM_SPEC = pl.BlockSpec(memory_space=pltpu.HBM)


def columns(ref, i):
    width = ref.shape[1] // PIECES
    return ref.at[:, i * width : (i + 1) * width]


def lines(ref, i):
    height = ref.shape[0] // PIECES
    return ref.at[i * height : (i + 1) * height]


def two_parts(refs, i):
    first, second = refs
    width = 2 * first.shape[1] // PIECES
    ref = first if i < PIECES // 2 else second
    i = i % (PIECES // 2)
    return ref.at[:, i * width : (i + 1) * width]


def fetch(*moves):
    copies = []
    for i in range(PIECES):
        copies.append(
            [
                pltpu.make_async_copy(
                    two_parts(source, i) if isinstance(source, tuple) else cut(source, i),
                    cut(here, i),
                    sems.at[i],
                )
                for cut, source, here, sems in moves
            ]
        )
        for copy in copies[-1]:
            copy.start()
    return copies


def finish(copies):
    for copy in copies:
        copy.wait()


def store(copies, here_ref, target_ref, sem):
    copies.append(pltpu.make_async_copy(here_ref, target_ref, sem))
    copies[-1].start()


def encode_kernel(
    dev_slots,
    capacity,
    bias_ref,
    rows_f_ref,
    rows_g_ref,
    enc_ref,
    dec_ref,
    code_ref,
    slopes_ref,
    partial_ref,
    rows_here,
    code_here,
    slopes_here,
    out_here,
    sems,
):
    slots, latents = slopes_here.shape
    copies = fetch((columns, (rows_f_ref, rows_g_ref), rows_here, sems.at[0]))
    preact = bias_ref[...]
    for i in range(PIECES):
        finish(copies[i])
        preact = preact + dot(columns(rows_here, i)[...], lines(enc_ref, i)[...], 1, 0)
    output, slopes = activate(preact)
    row = lax.broadcasted_iota(jnp.int32, (slots, latents), 0)
    latent = lax.broadcasted_iota(jnp.int32, (slots, latents), 1)
    own = lax.div(lax.rem(row, dev_slots), capacity) == lax.div(latent, BLOCK)
    code = jnp.where(own, output, 0.0).astype(BF16)
    stores = []
    code_here[...] = code
    store(stores, code_here, code_ref, sems.at[3, 0])
    slopes_here[...] = jnp.where(own, slopes, 0.0)
    store(stores, slopes_here, slopes_ref, sems.at[3, 1])
    for i in range(PIECES):
        columns(out_here, i)[...] = dot(code, columns(dec_ref, i)[...], 1, 0).astype(BF16)
        store(stores, columns(out_here, i), columns(partial_ref, i), sems.at[4, i])
    finish(stores)


def encode(dev_slots, capacity, rows, enc_weight, enc_bias, dec_weight):
    slots = rows[0].shape[0]
    features, latents = enc_weight.shape
    return pl.pallas_call(
        lambda *refs: encode_kernel(dev_slots, capacity, *refs),
        out_shape=[
            pltpu.HBM((slots, latents), BF16),
            pltpu.HBM((slots, latents), F32),
            pltpu.HBM((slots, features), BF16),
        ],
        in_specs=[VMEM_SPEC] + [HBM_SPEC] * 2 + [VMEM_SPEC] * 2,
        out_specs=[HBM_SPEC] * 3,
        scratch_shapes=[
            pltpu.VMEM((slots, features), BF16),
            pltpu.VMEM((slots, latents), BF16),
            pltpu.VMEM((slots, latents), F32),
            pltpu.VMEM((slots, features), BF16),
            pltpu.SemaphoreType.DMA((5, PIECES)),
        ],
        cost_estimate=pl.CostEstimate(
            flops=4 * slots * latents * features,
            bytes_accessed=4 * features * (slots + latents),
            transcendentals=slots * latents,
        ),
        compiler_params=pltpu.CompilerParams(vmem_limit_bytes=40 * MIB),
        name="encode",
    )(enc_bias, *rows, enc_weight, dec_weight)


def home_kernel(
    select_ref,
    select_t_ref,
    bias_ref,
    act_ref,
    returned_ref,
    full_ref,
    send_ref,
    act_here,
    here_ref,
    full_out_ref,
    send_out_ref,
    sems,
):
    moves = fetch(
        (columns, returned_ref, here_ref, sems.at[0]), (columns, act_ref, act_here, sems.at[3])
    )
    stores = []
    for i, copies in enumerate(moves):
        finish(copies)
        full = dot(select_t_ref[...], columns(here_ref, i)[...], 1, 0) + columns(bias_ref, i)[...]
        errors = (full - columns(act_here, i)[...].astype(F32)).astype(BF16)
        columns(send_out_ref, i)[...] = dot(select_ref[...], errors, 1, 0).astype(BF16)
        store(stores, columns(send_out_ref, i), columns(send_ref, i), sems.at[1, i])
        columns(full_out_ref, i)[...] = full.astype(BF16)
        store(stores, columns(full_out_ref, i), columns(full_ref, i), sems.at[2, i])
    finish(stores)


def rebuild(select, select_t, returned, activations, dec_bias):
    slots, tokens = select.shape
    features = activations.shape[1]
    return pl.pallas_call(
        home_kernel,
        out_shape=[
            pltpu.HBM((tokens, features), BF16),
            pltpu.HBM((slots, features), BF16),
        ],
        in_specs=[VMEM_SPEC] * 3 + [HBM_SPEC] * 2,
        out_specs=[HBM_SPEC, HBM_SPEC],
        scratch_shapes=[
            pltpu.VMEM((tokens, features), BF16),
            pltpu.VMEM((slots, features), BF16),
            pltpu.VMEM((tokens, features), BF16),
            pltpu.VMEM((slots, features), BF16),
            pltpu.SemaphoreType.DMA((4, PIECES)),
        ],
        cost_estimate=pl.CostEstimate(
            flops=4 * slots * tokens * features,
            bytes_accessed=4 * (slots + tokens) * features,
            transcendentals=0,
        ),
        compiler_params=pltpu.CompilerParams(vmem_limit_bytes=48 * MIB),
        name="rebuild",
    )(select, select_t, dec_bias, activations, returned)


def grads_kernel(
    count,
    squares_ref,
    code_t_ref,
    slopes_ref,
    dec_t_ref,
    rows_t_ref,
    got_ref,
    dec_grad_ref,
    enc_grad_ref,
    bias_grad_ref,
    code_t_here,
    slopes_here,
    dec_t_here,
    rows_t_here,
    got_here,
    dec_out,
    enc_out,
    sems,
):
    first = []
    store(first, code_t_ref, code_t_here, sems.at[5, 0])
    copies = fetch(
        (columns, got_ref, got_here, sems.at[0]),
        (lines, dec_t_ref, dec_t_here, sems.at[1]),
    )
    second = []
    store(second, slopes_ref, slopes_here, sems.at[5, 1])
    scale = LOSS_SCALE / (squares_ref[0:1, 0:1] / count + 1e-06)
    finish(first)
    stores = []
    code_grad = None
    for i in range(PIECES):
        finish(copies[i])
        if i == 1:
            rows_copies = fetch((lines, rows_t_ref, rows_t_here, sems.at[2]))
        got = columns(got_here, i)[...]
        columns(dec_out, i)[...] = (dot(code_t_here[...], got, 1, 0) * scale).astype(BF16)
        store(stores, columns(dec_out, i), columns(dec_grad_ref, i), sems.at[3, i])
        part = dot(got, lines(dec_t_here, i)[...], 1, 0)
        code_grad = part if i == 0 else code_grad + part
    finish(second)
    code_grad = code_grad * (slopes_here[...] * scale)
    bias_grad_ref[...] = jnp.sum(code_grad, axis=0, keepdims=True)
    code_grad = code_grad.astype(BF16)
    for i in range(PIECES):
        finish(rows_copies[i])
        lines(enc_out, i)[...] = dot(lines(rows_t_here, i)[...], code_grad, 1, 0).astype(BF16)
        store(stores, lines(enc_out, i), lines(enc_grad_ref, i), sems.at[4, i])
    finish(stores)


def gradients(count, squares, code_t, slopes, dec_t, rows_t, got_errors):
    latents, slots = code_t.shape
    features = dec_t.shape[0]
    return pl.pallas_call(
        lambda *refs: grads_kernel(count, *refs),
        out_shape=[
            pltpu.HBM((latents, features), BF16),
            pltpu.HBM((features, latents), BF16),
            jax.ShapeDtypeStruct((1, latents), F32),
        ],
        in_specs=[VMEM_SPEC] + [HBM_SPEC] * 5,
        out_specs=[HBM_SPEC, HBM_SPEC, VMEM_SPEC],
        scratch_shapes=[
            pltpu.VMEM((latents, slots), BF16),
            pltpu.VMEM((slots, latents), F32),
            pltpu.VMEM((features, latents), BF16),
            pltpu.VMEM((features, slots), BF16),
            pltpu.VMEM((slots, features), BF16),
            pltpu.VMEM((latents, features), BF16),
            pltpu.VMEM((features, latents), BF16),
            pltpu.SemaphoreType.DMA((6, PIECES)),
        ],
        cost_estimate=pl.CostEstimate(
            flops=6 * slots * latents * features,
            bytes_accessed=2 * features * (2 * slots + 3 * latents),
            transcendentals=0,
        ),
        compiler_params=pltpu.CompilerParams(vmem_limit_bytes=62 * MIB),
        name="gradients",
    )(squares, code_t, slopes, dec_t, rows_t, got_errors)


def per_device(activations, block_ids, enc_weight, enc_bias, dec_weight, dec_bias):
    tok_rows, feature_dim = activations.shape
    active_count = block_ids.shape[1]
    devices = lax.axis_size("lat")
    half = devices // 2
    local_latents = enc_weight.shape[1]
    blocks_dev = local_latents // BLOCK
    nblocks = blocks_dev * devices
    capacity = max(2, 3 * tok_rows * active_count // (2 * nblocks))
    dev_slots = blocks_dev * capacity
    half_slots = half * dev_slots
    side = feature_dim // 2

    def exchange(rows):
        return lax.all_to_all(rows, "lat", split_axis=0, concat_axis=0, tiled=True)

    def swap(rows, step=half):
        return lax.ppermute(rows, "lat", [(i, i ^ step) for i in range(devices)])

    def pick(select, rows):
        return dot(select, rows, 1, 0).astype(BF16)

    ids = block_ids.T
    order = jnp.arange(tok_rows, dtype=jnp.int32)
    same = jnp.any(ids[:, :, None, None] == ids.T[None, None, :, :], axis=3)
    same = same & (order[None, None, :] < order[None, :, None])
    slot_of = ids * capacity + jnp.sum(same.astype(jnp.int32), axis=2)
    slot_held = swap(slot_of)
    me = lax.axis_index("lat")
    slots = jnp.arange(2 * half_slots, dtype=jnp.int32)
    crossed = ((slots // dev_slots) ^ me) * dev_slots + slots % dev_slots

    def selection(slot, names):
        return jnp.any(names[:, None, None] == slot[None, :, :], axis=1).astype(BF16)

    select = selection(slot_of, slots)
    select_t = jnp.any(slots[None, None, :] == slot_of.T[:, :, None], axis=1).astype(BF16)
    select_own = selection(slot_of, crossed[:half_slots])
    select_held = selection(slot_held, crossed[:half_slots])
    by_swaps = half <= 8

    def deliver(tokens, by_slot_from, by_slot, value):
        if not by_swaps:
            return exchange(pick(select, tokens)), exchange(by_slot(by_slot_from)), value
        cuts = [slice(k * dev_slots, (k + 1) * dev_slots) for k in range(half)]
        own = [pick(select_own[cut], tokens) for cut in cuts]
        own = [own[0]] + list(together(*own[1:], by_slot_from))
        by_slot_from = own.pop()
        held = swap(tokens)
        got = exchange(by_slot(by_slot_from))
        held, value = together(held, value)
        rows = jnp.zeros((devices, dev_slots, tokens.shape[1]), BF16)
        far_first = list(range(half // 2, half)) + list(range(half // 2))
        for k in far_first:
            part = swap(own[k], k) if k else own[k]
            rows = lax.dynamic_update_index_in_dim(rows, part, me ^ k, 0)
        for k in far_first:
            part = pick(select_held[cuts[k]], held)
            part = swap(part, k) if k else part
            rows = lax.dynamic_update_index_in_dim(rows, part, me ^ (k + half), 0)
        return rows.reshape(devices * dev_slots, tokens.shape[1]), got, value

    act_f, act_g = activations[:, :side], activations[:, side:]
    rows_f, rows_g, squares = deliver(
        act_f, act_g, lambda rows: pick(select, rows), sum_of_squares(activations)
    )

    code_rows, slopes, partial_value = encode(
        dev_slots, capacity, (rows_f, rows_g), enc_weight, enc_bias[None, :], dec_weight
    )
    returned = exchange(partial_value)
    step = 1
    while step < devices:
        squares = squares + swap(squares, step)
        step *= 2
    returned, squares = together(returned, squares)
    full, send_errors = rebuild(select, select_t, returned, activations, dec_bias[None, :])
    send_errors, code_rows, rows_f, rows_g, dec_rows = together(
        send_errors, code_rows, rows_f, rows_g, dec_weight
    )
    got_errors = exchange(send_errors)
    dec_grad, enc_grad, bias_grad = gradients(
        tok_rows * devices * feature_dim,
        squares,
        code_rows.T,
        slopes,
        dec_rows.T,
        jnp.concatenate([rows_f.T, rows_g.T], axis=0),
        got_errors,
    )
    return (full, enc_grad, dec_grad, bias_grad.reshape(local_latents))


def solution(mesh):
    return jax.shard_map(
        per_device,
        mesh=mesh,
        in_specs=(
            P(("grp", "lat"), None),
            P(("grp", "lat"), None),
            P(None, "lat"),
            P("lat"),
            P("lat", None),
            P(),
        ),
        out_specs=(
            P(("grp", "lat"), None),
            P("grp", "lat"),
            P(("grp", "lat"), None),
            P(("grp", "lat")),
        ),
        check_vma=False,
    )
```
